256 devices in a mesh: grp: 64 (over z, y, core), tp: 4 (over x).
Axes of the slice: x: 4, y: 4, z: 8, core: 2. Of those that a mesh axis runs over, the one named last changes fastest.
Arguments:
- roll_query: bfloat16 [16384, 5120], P(('grp', 'tp')), may hold values from -6 to 6
- roll_key: bfloat16 [16384, 1024], P(('grp', 'tp')), may hold values from -6 to 6
- roll_value: bfloat16 [16384, 1024], P(('grp', 'tp')), may hold values from -6 to 6
- roll_cotangent: bfloat16 [16384, 5120], P(('grp', 'tp')), may hold values from -6 to 6
- route: int32 [16384], P(('grp', 'tp')), may hold values from 0 to 127, as said below
- arrival: int32 [16384], P('grp'), may hold values from 0 to 511, as said below
- lengths: int32 [64, 4], P('grp'), may hold values from 1 to 128, 256 in all within a row
- prefix_kv: bfloat16 [64, 512, 2, 1024], P('grp', None, None, 'tp'), may hold values from -6 to 6
- owner: int32 [16], replicated, may hold values from 0 to 3
Outputs:
- grad_query: bfloat16 [16384, 5120], P(('grp', 'tp'))
- grad_key: bfloat16 [16384, 1024], P(('grp', 'tp'))
- grad_value: bfloat16 [16384, 1024], P(('grp', 'tp'))
- grad_prefix: float32 [64, 512, 2, 1024], P('grp', None, None, 'tp')
The draws below stay inside these ranges and needn't reach their ends.
Inputs may be any that keep to these rules, and one draw needn't show every extreme that they name: `route`: each entry is t * 2 + s: the token goes to trainer t (a grp index) into slot s. The tokens of one rollout device sent to one trainer take slots 0, 1, ... without gaps, at most 2 of them; every device sends exactly 2 to some trainer, every trainer receives exactly 256 tokens and exactly 2 from some device. `arrival`: entry t * 256 + j is r * 8 + p * 2 + s for the token that the rollout device with grp index r and tp index p sends to trainer t into slot s; the 256 entries of a trainer name each token sent to it once.
All inputs are finite; a program needn't handle non-finite values.
Results may differ from the reference program's by a relative error of at most 0.0073.
Values may be sent and summed in bfloat16 or wider, within the bound.
A program may use at most 64 MiB of HBM per device.

```python
import math
import jax
import jax.numpy as jnp
import numpy as np
from jax import lax

HEADS = 40
KV_HEADS = 8
HEAD_DIM = 128
TRAINERS = 4
ROWS = 256
PREFIX = 512
CPT = 4
LEN = 128
ROLL_ROWS = 64
CAP = 2
ALL_ROWS = 16384
GROUPS = 16
N_GRP = 64
N_TP = 4


def routing_tables(key):
    key = jax.random.fold_in(key, 101)
    keys_all = jax.random.split(key, 5)
    mean_load = ROLL_ROWS // N_GRP
    half_count = N_GRP // 2
    offsets = jax.random.randint(keys_all[0], (N_TP, half_count), 0, mean_load + 1)
    offsets = offsets.at[:, 0].set(mean_load)
    base_load = jnp.concatenate([mean_load + offsets, mean_load - offsets], axis=1).astype(jnp.int32)
    shuffle_dest = jax.vmap(lambda sub_key: jax.random.permutation(sub_key, N_GRP))(jax.random.split(keys_all[1], N_TP))
    shuffle_src = jax.vmap(lambda sub_key: jax.random.permutation(sub_key, N_GRP))(jax.random.split(keys_all[2], N_TP))
    lookup = (shuffle_dest[:, None, :] + shuffle_src[:, :, None]) % N_GRP
    counts = jnp.take_along_axis(jnp.broadcast_to(base_load[:, None, :], lookup.shape), lookup, axis=2)
    inclusive = jnp.cumsum(counts, axis=2)
    exclusive = inclusive - counts
    row_index = jnp.arange(ROLL_ROWS, dtype=jnp.int32)
    destination = jnp.sum((inclusive[:, :, :, None] <= row_index).astype(jnp.int32), axis=2)
    slot_index = row_index - jnp.take_along_axis(exclusive, destination, axis=2)
    route_code = jnp.transpose(destination * CAP + slot_index, (1, 0, 2)).reshape(N_GRP * N_TP, ROLL_ROWS)
    orders = jax.vmap(lambda sub_key: jax.random.permutation(sub_key, ROLL_ROWS))(jax.random.split(keys_all[3], N_GRP * N_TP))
    route_table = jnp.take_along_axis(route_code, orders, axis=1).reshape(-1).astype(jnp.int32)
    slot_range = jnp.arange(CAP, dtype=jnp.int32)
    received = jnp.transpose(counts, (2, 1, 0))
    slot_total = N_GRP * N_TP * CAP
    filled = (slot_range[None, None, None, :] < received[:, :, :, None]).reshape(N_GRP, slot_total)
    rank_table = jax.vmap(lambda sub_key: jax.random.permutation(sub_key, slot_total))(jax.random.split(keys_all[4], N_GRP))
    scores_int = rank_table + jnp.where(filled, 0, slot_total)
    chosen = jnp.argsort(scores_int, axis=1)[:, :ROWS].astype(jnp.int32)
    return (route_table, chosen.reshape(-1))


def draw_route(key, part):
    return routing_tables(key)[0]


def draw_arrival(key, part):
    return routing_tables(key)[1]


def draw_roll_query(key, part):
    key = jax.random.fold_in(key, 3)
    keys_all = jax.random.split(key, 1)
    row_total = N_GRP * ROWS
    base_value = jnp.clip(jax.random.normal(keys_all[0], (row_total, HEADS * HEAD_DIM), jnp.float32), -6.0, 6.0)
    return base_value.astype(jnp.bfloat16)


def draw_prefix_kv(key, part):
    key = jax.random.fold_in(key, 5)
    keys_all = jax.random.split(key, 1)
    shape = (N_GRP, PREFIX, 2, KV_HEADS * HEAD_DIM)
    base_value = jnp.clip(jax.random.normal(keys_all[0], shape, jnp.float32), -6.0, 6.0)
    return base_value.astype(jnp.bfloat16)


def with_ends(values, rng, least, largest):
    extent = values.shape
    place = [jax.random.randint(jax.random.fold_in(rng, axis), (), 0, extent[axis]) for axis in range(len(extent))]
    values = values.at[tuple(place)].set(least)
    longest = extent.index(max(extent))
    place[longest] = (place[longest] + 1) % extent[longest]
    return values.at[tuple(place)].set(largest)


def shard_levels(own_key, extent, pieces, smallest, high):
    level, own = 1.0, jax.random.fold_in(own_key, 6)
    for dim, blocks in pieces:
        heights = jnp.exp(jax.random.uniform(jax.random.fold_in(own, dim), (blocks,), jnp.float32, smallest / len(pieces), high / len(pieces)))
        level = level * jnp.repeat(heights, extent[dim] // blocks).reshape([-1 if axis == dim else 1 for axis in range(len(extent))])
    return level


def length_profile(count, total, reach, skew):
    portions = [(1 << 20) // math.isqrt(standing ** skew) + 1 for standing in range(2, count + 1)]
    rest, given = total - reach - (count - 1), [1] * (count - 1)
    while rest > 0:
        free = [i for i in range(count - 1) if given[i] < reach]
        mass, budget = sum([portions[i] for i in free]), rest
        for i in free:
            extra = min(reach - given[i], max(1, budget * portions[i] // mass), rest)
            given[i] = given[i] + extra
            rest = rest - extra
    return np.array([reach] + given)


def uneven(rng, amount, total, limit, slope):
    if amount == 2:
        one = jax.random.randint(rng, (), max(1, total - limit), min(limit, total - 1) + 1)
        return jnp.stack([one, total - one])
    tallies = jnp.asarray(length_profile(amount, total, limit, slope), jnp.int32)
    twos = (amount - 1) // 2
    donor, receiver = tallies[1:1 + 2 * twos:2], tallies[2:2 + 2 * twos:2]
    room = jnp.minimum(donor - 1, limit - receiver)
    shifted = jax.random.randint(jax.random.fold_in(rng, 1), (twos,), 0, 1 << 20) % (room + 1)
    tallies = tallies.at[1:1 + 2 * twos:2].set(donor - shifted).at[2:2 + 2 * twos:2].set(receiver + shifted)
    return tallies[jax.random.permutation(jax.random.fold_in(rng, 2), amount)]


def noise(key, shape, spread, bound, cuts=(), kind=jnp.bfloat16):
    result = jax.random.normal(key, shape, jnp.float32) * spread
    if len(cuts) > 0:
        result = shard_levels(key, shape, cuts, -0.22, 0.18) * result
    return jnp.clip(result, min=-bound, max=bound).astype(kind)


def setup_inputs(seed: int = 0) -> dict:
    seeds = jax.random.split(jax.random.key(seed), 10)
    return {
        "roll_query": draw_roll_query(jax.random.fold_in(seeds[9], 71), 0),
        "roll_key": noise(seeds[1], (ALL_ROWS, KV_HEADS * HEAD_DIM), 1.0, 6.0, ((0, 256),)),
        "roll_value": noise(seeds[2], (ALL_ROWS, KV_HEADS * HEAD_DIM), 1.0, 6.0, ((0, 256),)),
        "roll_cotangent": noise(seeds[3], (ALL_ROWS, HEADS * HEAD_DIM), 1.0, 6.0, ((0, 256),)),
        "route": draw_route(jax.random.fold_in(seeds[9], 71), 0),
        "arrival": draw_arrival(jax.random.fold_in(seeds[9], 71), 0),
        "lengths": jax.vmap(lambda own: uneven(own, CPT, ROWS, LEN, 1))(jax.random.split(seeds[6], N_GRP)).reshape((N_GRP, CPT)).astype(jnp.int32),
        "prefix_kv": draw_prefix_kv(jax.random.fold_in(seeds[9], 71), 0),
        "owner": with_ends(jax.random.randint(seeds[8], (GROUPS,), 0, TRAINERS), jax.random.fold_in(seeds[8], 1), 0, TRAINERS - 1).astype(jnp.int32),
    }


NEGATIVE = -1e+30

def completion_mask(length_row, row_count, prefix_count):
    row_index = jnp.arange(row_count, dtype=jnp.int32)
    finish = jnp.cumsum(length_row).astype(jnp.int32)
    starts = finish - length_row
    completion = lax.optimization_barrier(jnp.sum((row_index[:, None] >= finish[None, :]).astype(jnp.int32), axis=1))
    member_of = completion[:, None] == jnp.arange(length_row.shape[0], dtype=jnp.int32)[None, :]
    position = row_index - lax.optimization_barrier(jnp.sum(jnp.where(member_of, starts[None, :], 0), axis=1))
    same_completion = completion[:, None] == completion[None, :]
    causal = position[None, :] <= position[:, None]
    prefix_part = jnp.ones((row_count, prefix_count), jnp.bool_)
    return jnp.concatenate([prefix_part, same_completion & causal], axis=1)

def attend_all(queries, comp_keys, comp_values, cotangent, prefix_keys, prefix_values, allowed):
    row_count = queries.shape[0]
    prefix_count = prefix_keys.shape[0]
    key_heads = comp_keys.shape[1] // HEAD_DIM
    head_ratio = queries.shape[1] // comp_keys.shape[1]
    score_scale = 1.0 / math.sqrt(HEAD_DIM)
    all_keys = jnp.concatenate([prefix_keys, comp_keys], 0).reshape(-1, key_heads, HEAD_DIM).astype(jnp.float32)
    all_values = jnp.concatenate([prefix_values, comp_values], 0).reshape(-1, key_heads, HEAD_DIM).astype(jnp.float32)
    query_heads = queries.reshape(row_count, key_heads, head_ratio, HEAD_DIM).astype(jnp.float32)
    grad_out = cotangent.reshape(row_count, key_heads, head_ratio, HEAD_DIM).astype(jnp.float32)
    scores = jnp.einsum('rhgd,khd->hgrk', query_heads, all_keys) * score_scale
    scores = jnp.where(allowed[None, None], scores, NEGATIVE)
    row_peak = lax.optimization_barrier(jnp.max(scores, axis=-1, keepdims=True))
    weights = jnp.exp(scores - row_peak)
    probability = weights / lax.optimization_barrier(jnp.sum(weights, axis=-1, keepdims=True))
    prob_bf = lax.optimization_barrier(probability.astype(jnp.bfloat16)).astype(jnp.float32)
    attended = jnp.einsum('hgrk,khd->rhgd', prob_bf, all_values)
    row_delta = lax.optimization_barrier(jnp.sum(grad_out * attended, axis=-1))
    grad_prob = jnp.einsum('rhgd,khd->hgrk', grad_out, all_values)
    dscore = probability * (grad_prob - jnp.transpose(row_delta, (1, 2, 0))[..., None])
    dscore_bf = lax.optimization_barrier(dscore.astype(jnp.bfloat16)).astype(jnp.float32)
    query_grad = (jnp.einsum('hgrk,khd->rhgd', dscore_bf, all_keys) * score_scale).astype(jnp.bfloat16)
    key_grad = (jnp.einsum('hgrk,rhgd->khd', dscore_bf, query_heads) * score_scale).reshape(-1, key_heads * HEAD_DIM)
    value_grad = jnp.einsum('hgrk,rhgd->khd', prob_bf, grad_out).reshape(-1, key_heads * HEAD_DIM)
    return (query_grad.reshape(row_count, -1), key_grad[prefix_count:].astype(jnp.bfloat16), value_grad[prefix_count:].astype(jnp.bfloat16), key_grad[:prefix_count], value_grad[:prefix_count])

def reference(roll_query, roll_key, roll_value, roll_cotangent, route, arrival, lengths, prefix_kv, owner):
    global_row = jnp.arange(ALL_ROWS, dtype=jnp.int32)
    device = global_row // ROLL_ROWS
    sender_group = device // N_TP
    sender_tp = device % N_TP
    destination = route // CAP
    slot_index = route % CAP
    slot_span = N_GRP * N_TP * CAP
    keycode = destination * slot_span + sender_group * (N_TP * CAP) + sender_tp * CAP + slot_index
    lookup_table = jnp.zeros((N_GRP * slot_span,), jnp.int32).at[keycode].set(global_row)
    trainer_of = global_row // ROWS
    source = lookup_table[trainer_of * slot_span + arrival]

    def one_trainer(trainer):
        picked = lax.dynamic_slice_in_dim(source, trainer * ROWS, ROWS)
        group_index = trainer // TRAINERS
        holder = group_index * TRAINERS + owner[group_index]
        prefix_keys = prefix_kv[holder, :, 0]
        prefix_values = prefix_kv[holder, :, 1]
        allowed = completion_mask(lengths[trainer], ROWS, PREFIX)
        return attend_all(roll_query[picked], roll_key[picked], roll_value[picked], roll_cotangent[picked], prefix_keys, prefix_values, allowed)
    query_grad, key_grad, value_grad, prefix_key_grad, prefix_value_grad = lax.map(one_trainer, jnp.arange(N_GRP, dtype=jnp.int32))
    grad_query = jnp.zeros((ALL_ROWS, HEADS * HEAD_DIM), jnp.bfloat16).at[source].set(query_grad.reshape(ALL_ROWS, -1))
    grad_key = jnp.zeros((ALL_ROWS, KV_HEADS * HEAD_DIM), jnp.bfloat16).at[source].set(key_grad.reshape(ALL_ROWS, -1))
    grad_value = jnp.zeros((ALL_ROWS, KV_HEADS * HEAD_DIM), jnp.bfloat16).at[source].set(value_grad.reshape(ALL_ROWS, -1))
    stacked = jnp.stack([prefix_key_grad, prefix_value_grad], axis=2)
    summed = lax.optimization_barrier(jnp.sum(stacked.reshape(GROUPS, TRAINERS, PREFIX, 2, KV_HEADS * HEAD_DIM), axis=1))
    chosen = (jnp.arange(TRAINERS, dtype=jnp.int32)[None, :] == owner[:, None]).astype(jnp.float32)
    grad_prefix = (chosen[:, :, None, None, None] * summed[:, None]).reshape(N_GRP, PREFIX, 2, KV_HEADS * HEAD_DIM)
    return (grad_query, grad_key, grad_value, grad_prefix)
```

```python
import functools
import math

import jax
import jax.numpy as jnp
from jax import lax
from jax.experimental import pallas as pl
from jax.experimental.pallas import tpu as pltpu
from jax.sharding import PartitionSpec as P

MESH = pl.DeviceIdType.MESH
D = 128
TP = 4
PLANE = 8
RATIO = 5
KH = 2
ROWS = 256
SEND = 64
PRE = 512
CHUNKS = 6
WIDE = 512
BACKS = 8
BACK = 256
PITCH = 128
NEGATIVE = -1e30
SCALE = 1.0 / math.sqrt(D)
F32 = jnp.float32
BF16 = jnp.bfloat16
I32 = jnp.int32
WIDTHS = (128, 256, 256, 256)


def iota(shape, dim):
    return lax.broadcasted_iota(I32, shape, dim)


def hot(match):
    return jnp.where(match, 1.0, 0.0).astype(BF16)


def dot(a, b):
    return jnp.dot(a, b, preferred_element_type=F32)


def dot_nt(a, b):
    return lax.dot_general(a, b, (((1,), (1,)), ((), ())), preferred_element_type=F32)


def place(kind, valid, lanes, limit):
    classes = iota((8, lanes), 0)
    member = (kind == classes) & valid
    before = hot(iota((lanes, lanes), 0) < iota((lanes, lanes), 1))
    count = dot(hot(member), before)
    rank = jnp.sum(jnp.where(member, count, 0.0), axis=0, keepdims=True).astype(I32)
    kind, valid = kind[0:1], valid[0:1]
    slot = jnp.where(valid & (rank < limit), kind * limit + rank, -1)
    table = jnp.where(valid & (rank < limit), kind * PITCH + rank, -1)
    return slot, table


def tabulate(code, table, lanes):
    sub = iota((8, lanes), 0)
    high, low = code >> 7, code & 127
    parts = jnp.where(sub == 0, high, jnp.where(sub == 1, low, 0)).astype(F32).astype(BF16)
    spread = hot(iota((8 * PITCH, lanes), 0) == table)
    return dot_nt(parts, spread)


def compacted(table, limit):
    lanes = 8 * limit
    lane = iota((8 * PITCH, lanes), 1)
    target = lane
    for i in range(1, 8):
        target = target + jnp.where(lane >= i * limit, PITCH - limit, 0)
    pick = hot(iota((8 * PITCH, lanes), 0) == target)
    parts = dot(table.astype(BF16), pick)
    return (parts[0:1] * 128.0 + parts[1:2]).astype(I32)


def turned(matrix):
    n = matrix.shape[1]
    eye = hot(iota((n, n), 0) == iota((n, n), 1))
    return dot_nt(eye, matrix).astype(BF16)


def kernel(
    cap_y,
    cap_z,
    query,
    key,
    value,
    cotangent,
    route,
    arrival,
    lengths,
    prefix,
    holder,
    grad_query,
    grad_key,
    grad_value,
    grad_prefix,
    x_table,
    y_table_out,
    y_table_in,
    z_table_out,
    z_table_in,
    x_in,
    y_out,
    y_in,
    z_out,
    z_in,
    bz_out,
    bz_in,
    by_out,
    by_in,
    bx_out,
    pre_in,
    pre_now,
    pre_far,
    to_y,
    to_z,
    to_rows,
    from_y,
    from_z,
    from_rows,
    mask,
    acc,
    acc_in,
    chip,
    chip_in,
    total,
    t_send,
    t_recv,
    x_send,
    x_recv,
    y_send,
    y_recv,
    z_send,
    z_recv,
    bz_send,
    bz_recv,
    by_send,
    by_recv,
    bx_send,
    bx_recv,
    p_send,
    p_recv,
    a_send,
    a_recv,
):
    grp = lax.axis_index("grp")
    tp = lax.axis_index("tp")
    plane = grp // PLANE
    spot = lax.rem(grp, PLANE)
    core = lax.rem(spot, 2)
    side = lax.rem(spot // 2, 2)
    mate = grp + 1 - 2 * core
    across = grp + 2 - 4 * side

    def x_peer(k):
        return lax.rem(tp + k, TP)

    def y_peer(k):
        return lax.rem(spot + k, PLANE)

    def z_peer(k):
        return lax.rem(plane + k, PLANE)

    def at_x(k):
        return (grp, x_peer(k))

    def at_y(k):
        return (plane * PLANE + y_peer(k), tp)

    def at_z(k):
        return (z_peer(k) * PLANE + spot, tp)

    def block(index, size):
        return pl.ds(pl.multiple_of(index * size, size), size)

    def remote(src, dst, send, recv, device):
        copy = pltpu.make_async_remote_copy(
            src_ref=src,
            dst_ref=dst,
            send_sem=send,
            recv_sem=recv,
            device_id=device,
            device_id_type=MESH,
        )
        copy.start()
        return copy

    def local(src, dst, sem):
        pltpu.make_async_copy(src, dst, sem).start()

    def await_bytes(ref, sem):
        pltpu.make_async_copy(ref, ref, sem).wait()

    entry = pltpu.get_barrier_semaphore()
    for k in range(1, TP):
        pl.semaphore_signal(entry, inc=1, device_id=at_x(k), device_id_type=MESH)
    for k in range(1, PLANE):
        pl.semaphore_signal(entry, inc=1, device_id=at_y(k), device_id_type=MESH)
    for k in range(1, PLANE):
        pl.semaphore_signal(entry, inc=1, device_id=at_z(k), device_id_type=MESH)
    pl.semaphore_wait(entry, TP - 1 + 2 * (PLANE - 1))

    for k in range(1, TP):
        remote(route, x_table.at[k - 1], t_send.at[0], t_recv.at[0], at_x(k))

    def chunk_parts(chunk, to):
        kh, part = chunk // 3, chunk % 3
        head = to * (KH * RATIO) + kh * RATIO
        if part == 0:
            return (
                (key, to * KH + kh, 1),
                (value, to * KH + kh, 1),
                (query, head, 1),
                (cotangent, head, 1),
            )
        first = head + 2 * part - 1
        return ((query, first, 2), (cotangent, first, 2))

    def x_stage(chunk):
        for k in range(TP):
            to = x_peer(k)
            lane = 0
            for source, head, heads in chunk_parts(chunk, to):
                src = source.at[:, pl.ds(pl.multiple_of(head * D, D), heads * D)]
                dst = x_in.at[chunk, block(tp, SEND), pl.ds(lane, heads * D)]
                if k == 0:
                    local(src, dst, x_recv.at[chunk])
                else:
                    remote(src, dst, x_send.at[chunk], x_recv.at[chunk], at_x(k))
                lane += heads * D

    x_stage(0)
    remote(prefix, pre_in, p_send.at[0], p_recv.at[0], (mate, tp))
    for chunk in range(1, CHUNKS):
        x_stage(chunk)

    await_bytes(x_table, t_recv.at[0])
    routes = route[...] + x_table[0] + x_table[1] + x_table[2]
    trainer = routes >> 1
    line = iota((8, ROWS), 1) // SEND
    number = grp * (2 * TP) + line * 2 + (routes & 1)
    code = ((trainer >> 3) * 512 + number + 1)[0:1]
    slot, table = place(trainer & 7, trainer >= 0, ROWS, cap_y)
    to_y[...] = hot(iota((8 * cap_y, ROWS), 0) == slot)
    y_table_out[...] = tabulate(code, table, ROWS)
    for k in range(1, PLANE):
        remote(
            y_table_out.at[:, block(y_peer(k), PITCH)],
            y_table_in.at[:, block(spot, PITCH)],
            t_send.at[1],
            t_recv.at[1],
            at_y(k),
        )
    local(
        y_table_out.at[:, block(spot, PITCH)], y_table_in.at[:, block(spot, PITCH)], t_recv.at[1]
    )

    def y_stage(chunk):
        await_bytes(x_in.at[chunk], x_recv.at[chunk])
        y_out[chunk] = dot(to_y[...], x_in[chunk]).astype(BF16)
        for k in range(1, PLANE):
            remote(
                y_out.at[chunk, block(y_peer(k), cap_y)],
                y_in.at[chunk, block(spot, cap_y)],
                y_send.at[chunk],
                y_recv.at[chunk],
                at_y(k),
            )
        local(
            y_out.at[chunk, block(spot, cap_y)],
            y_in.at[chunk, block(spot, cap_y)],
            y_recv.at[chunk],
        )

    def z_stage(chunk):
        await_bytes(y_in.at[chunk], y_recv.at[chunk])
        z_out[chunk] = dot(to_z[...], y_in[chunk]).astype(BF16)
        for k in (4, 3, 5, 2, 6, 1, 7):
            remote(
                z_out.at[chunk, block(z_peer(k), cap_z)],
                z_in.at[chunk, block(plane, cap_z)],
                z_send.at[chunk],
                z_recv.at[chunk],
                at_z(k),
            )
        local(
            z_out.at[chunk, block(plane, cap_z)],
            z_in.at[chunk, block(plane, cap_z)],
            z_recv.at[chunk],
        )

    y_stage(0)
    y_stage(1)

    await_bytes(y_table_in, t_recv.at[1])
    code = compacted(y_table_in[...], cap_y)
    lanes = 8 * cap_y
    code8 = jnp.broadcast_to(code, (8, lanes))
    slot, table = place((code8 - 1) >> 9, code8 > 0, lanes, cap_z)
    to_z[...] = hot(iota((8 * cap_z, lanes), 0) == slot)
    z_table_out[...] = tabulate(((code - 1) & 511) + 1, table, lanes)
    for k in range(1, PLANE):
        remote(
            z_table_out.at[:, block(z_peer(k), PITCH)],
            z_table_in.at[:, block(plane, PITCH)],
            t_send.at[2],
            t_recv.at[2],
            at_z(k),
        )
    local(
        z_table_out.at[:, block(plane, PITCH)], z_table_in.at[:, block(plane, PITCH)], t_recv.at[2]
    )

    z_stage(0)

    hold = holder[0:1, :]
    await_bytes(pre_in, p_recv.at[0])
    mine = (hold & 1) == core
    pre_now[...] = jnp.where(
        mine, prefix[...].astype(F32), pre_in[...].astype(F32)
    ).astype(BF16)
    remote(
        pre_now.at[block(core, 2 * PRE)],
        pre_far.at[block(core, 2 * PRE)],
        p_send.at[1],
        p_recv.at[1],
        (across, tp),
    )

    y_stage(2)
    z_stage(1)
    y_stage(3)
    z_stage(2)
    await_bytes(pre_far.at[block(core, 2 * PRE)], p_recv.at[1])
    remote(
        pre_far.at[block(core, 2 * PRE)],
        pre_far.at[block(core, 2 * PRE)],
        p_send.at[2],
        p_recv.at[2],
        (mate, tp),
    )
    y_stage(4)
    z_stage(3)
    y_stage(5)
    z_stage(4)
    z_stage(5)

    ends = [lengths[0:1, :]]
    for i in range(1, 3):
        ends.append(ends[-1] + lengths[i : i + 1, :])
    query_row = iota((ROWS, ROWS), 1)
    key_row = iota((ROWS, ROWS), 0)
    same = key_row <= query_row
    for end in ends:
        end = jnp.concatenate([end, end], axis=1)
        same = same & ((key_row >= end) == (query_row >= end))
    mask[...] = jnp.where(same, 0.0, NEGATIVE)
    await_bytes(pre_far.at[block(1 - core, 2 * PRE)], p_recv.at[2])
    await_bytes(pre_now.at[pl.ds(0, 2 * PRE)], p_send.at[1])
    here = (hold >> 1) == side
    pre_now[...] = jnp.where(
        here, pre_now[...].astype(F32), pre_far[...].astype(F32)
    ).astype(BF16)
    from_y[...] = turned(to_y[...])
    from_z[...] = turned(to_z[...])

    await_bytes(z_table_in, t_recv.at[2])
    code = compacted(z_table_in[...], cap_z) - 1
    rows = hot(arrival[:, 0:1] == code)
    to_rows[...] = rows
    from_rows[...] = turned(rows)

    def back_z(chunk, result):
        wide = result.shape[1]
        lanes = pl.ds(0, wide)
        bz_out[chunk, :, 0:wide] = dot(from_rows[...], result).astype(BF16)
        for k in (4, 3, 5, 2, 6, 1, 7):
            remote(
                bz_out.at[chunk, block(z_peer(k), cap_z), lanes],
                bz_in.at[chunk, block(plane, cap_z), lanes],
                bz_send.at[chunk],
                bz_recv.at[chunk],
                at_z(k),
            )
        local(
            bz_out.at[chunk, block(plane, cap_z), lanes],
            bz_in.at[chunk, block(plane, cap_z), lanes],
            bz_recv.at[chunk],
        )

    def back_y(chunk):
        wide = WIDTHS[chunk % 4]
        lanes = pl.ds(0, wide)
        await_bytes(bz_in.at[chunk, :, lanes], bz_recv.at[chunk])
        by_out[chunk, :, 0:wide] = dot(from_z[...], bz_in[chunk, :, 0:wide]).astype(BF16)
        for k in range(1, PLANE):
            remote(
                by_out.at[chunk, block(y_peer(k), cap_y), lanes],
                by_in.at[chunk, block(spot, cap_y), lanes],
                by_send.at[chunk],
                by_recv.at[chunk],
                at_y(k),
            )
        local(
            by_out.at[chunk, block(spot, cap_y), lanes],
            by_in.at[chunk, block(spot, cap_y), lanes],
            by_recv.at[chunk],
        )

    def back_x(chunk):
        kh, part = chunk // 4, chunk % 4
        wide = WIDTHS[part]
        lanes = pl.ds(0, wide)
        await_bytes(by_in.at[chunk, :, lanes], by_recv.at[chunk])
        bx_out[chunk, :, 0:wide] = dot(from_y[...], by_in[chunk, :, 0:wide]).astype(BF16)
        head = tp * (KH * RATIO) + kh * RATIO
        if part < 3:
            first = head if part == 0 else head + 2 * part - 1
            parts = ((grad_query, first, wide // D),)
        else:
            parts = ((grad_key, tp * KH + kh, 1), (grad_value, tp * KH + kh, 1))
        for k in range(TP):
            lane = 0
            for target, head, heads in parts:
                src = bx_out.at[chunk, block(x_peer(k), SEND), pl.ds(lane, heads * D)]
                dst = target.at[:, pl.ds(pl.multiple_of(head * D, D), heads * D)]
                if k == 0:
                    local(src, dst, bx_recv.at[chunk])
                else:
                    remote(src, dst, bx_send.at[chunk], bx_recv.at[chunk], at_x(k))
                lane += heads * D

    def reduce_core(kh):
        remote(acc.at[kh, 1 - core], acc_in.at[kh], a_send.at[kh, 0], a_recv.at[kh, 0], (mate, tp))

    def reduce_side(kh):
        await_bytes(acc_in.at[kh], a_recv.at[kh, 0])
        chip[kh] = acc[kh, core] + acc_in[kh]
        remote(chip.at[kh], chip_in.at[kh], a_send.at[kh, 1], a_recv.at[kh, 1], (across, tp))

    def reduce_end(kh):
        await_bytes(chip_in.at[kh], a_recv.at[kh, 1])
        whole = chip[kh] + chip_in[kh]
        total[kh, 0] = jnp.where(hold == 2 * side + core, whole, 0.0)
        total[kh, 1] = jnp.where(hold == 2 * side + 1 - core, whole, 0.0)
        local(total.at[kh, 0], grad_prefix.at[core, kh], a_recv.at[kh, 2])
        remote(
            total.at[kh, 1], grad_prefix.at[core, kh], a_send.at[kh, 2], a_recv.at[kh, 3], (mate, tp)
        )

    def tokens(chunk):
        await_bytes(z_in.at[chunk], z_recv.at[chunk])
        return dot(to_rows[...], z_in[chunk]).astype(BF16)

    def attend(keys, values, keys_t, queries, grads, key_grad, value_grad):
        scores = dot_nt(keys, queries) * SCALE
        scores = jnp.concatenate([scores[:PRE], scores[PRE:] + mask[...]], axis=0)
        weights = jnp.exp(scores - jnp.max(scores, axis=0, keepdims=True))
        probability = weights * (1.0 / jnp.sum(weights, axis=0, keepdims=True))
        grad_prob = dot_nt(values, grads)
        delta = jnp.sum(probability * grad_prob, axis=0, keepdims=True)
        dscore = (probability * (grad_prob - delta)).astype(BF16)
        key_part = dot(dscore, queries)
        value_part = dot(probability.astype(BF16), grads)
        query_grad = (jnp.transpose(dot(keys_t, dscore)) * SCALE).astype(BF16)
        if key_grad is None:
            return query_grad, key_part, value_part
        return query_grad, key_grad + key_part, value_grad + value_part

    later = []
    for kh in range(KH):
        base = kh * 3
        got = tokens(base)
        lower = kh * PRE
        keys = jnp.concatenate([pre_now[lower : lower + PRE], got[:, 0:D]], axis=0)
        values = jnp.concatenate(
            [pre_now[KH * PRE + lower : KH * PRE + lower + PRE], got[:, D : 2 * D]], axis=0
        )
        keys_t = jnp.transpose(keys.astype(F32)).astype(BF16)
        key_grad = value_grad = None
        for part in range(3):
            if part == 0:
                pairs = ((got[:, 2 * D : 3 * D], got[:, 3 * D :]),)
            else:
                got = tokens(base + part)
                pairs = ((got[:, :D], got[:, 2 * D : 3 * D]), (got[:, D : 2 * D], got[:, 3 * D :]))
            results = []
            for queries, grads in pairs:
                result, key_grad, value_grad = attend(
                    keys, values, keys_t, queries, grads, key_grad, value_grad
                )
                results.append(result)
            whole = results[0] if part == 0 else jnp.concatenate(results, axis=1)
            back_z(kh * 4 + part, whole)
            if kh == 1:
                back_y(part)
                if part > 0:
                    back_x(part - 1)
        own = [(key_grad[PRE:] * SCALE).astype(BF16), value_grad[PRE:].astype(BF16)]
        back_z(kh * 4 + 3, jnp.concatenate(own, axis=1))
        acc[kh, 0] = key_grad[:PRE] * SCALE
        acc[kh, 1] = value_grad[:PRE]
        reduce_core(kh)
        if kh == 1:
            reduce_side(0)

    back_y(3)
    back_x(2)
    reduce_side(1)
    back_y(4)
    back_x(3)
    reduce_end(0)
    back_y(5)
    back_x(4)
    back_y(6)
    back_x(5)
    reduce_end(1)
    back_y(7)
    back_x(6)
    back_x(7)

    for i in range(TP - 1):
        await_bytes(route, t_send.at[0])
    for i, ref in ((1, y_table_out), (2, z_table_out)):
        await_bytes(ref.at[:, pl.ds(0, 7 * PITCH)], t_send.at[i])
    for chunk in range(CHUNKS):
        await_bytes(x_in.at[chunk, pl.ds(0, 3 * SEND)], x_send.at[chunk])
        await_bytes(y_out.at[chunk, pl.ds(0, 7 * cap_y)], y_send.at[chunk])
        await_bytes(z_out.at[chunk, pl.ds(0, 7 * cap_z)], z_send.at[chunk])
    for chunk in range(BACKS):
        lanes = pl.ds(0, WIDTHS[chunk % 4])
        await_bytes(bz_out.at[chunk, pl.ds(0, 7 * cap_z), lanes], bz_send.at[chunk])
        await_bytes(by_out.at[chunk, pl.ds(0, 7 * cap_y), lanes], by_send.at[chunk])
        await_bytes(bx_out.at[chunk, pl.ds(0, 3 * SEND), lanes], bx_send.at[chunk])
        await_bytes(bx_out.at[chunk, :, lanes], bx_recv.at[chunk])
    await_bytes(prefix, p_send.at[0])
    await_bytes(pre_now.at[pl.ds(0, 2 * PRE)], p_send.at[2])
    for kh in range(KH):
        await_bytes(acc_in.at[kh], a_send.at[kh, 0])
        await_bytes(chip.at[kh], a_send.at[kh, 1])
        await_bytes(chip.at[kh], a_send.at[kh, 2])
        await_bytes(chip.at[kh], a_recv.at[kh, 2])
        await_bytes(chip.at[kh], a_recv.at[kh, 3])


def whole_step(cap_y, cap_z, operands):
    def vmem(*shape, dtype=BF16):
        return pltpu.VMEM(shape, dtype)

    dma = pltpu.SemaphoreType.DMA
    in_vmem = pl.BlockSpec(memory_space=pltpu.VMEM)
    anywhere = pl.BlockSpec(memory_space=pl.ANY)
    return pl.pallas_call(
        functools.partial(kernel, cap_y, cap_z),
        out_shape=(
            jax.ShapeDtypeStruct((SEND, TP * KH * RATIO * D), BF16),
            jax.ShapeDtypeStruct((SEND, TP * KH * D), BF16),
            jax.ShapeDtypeStruct((SEND, TP * KH * D), BF16),
            jax.ShapeDtypeStruct((2, KH, PRE, D), F32),
        ),
        in_specs=[anywhere] * 4 + [in_vmem] * 5,
        out_specs=(anywhere,) * 4,
        scratch_shapes=[
            vmem(TP - 1, 8, ROWS, dtype=I32),
            vmem(8, 8 * PITCH, dtype=F32),
            vmem(8, 8 * PITCH, dtype=F32),
            vmem(8, 8 * PITCH, dtype=F32),
            vmem(8, 8 * PITCH, dtype=F32),
            vmem(CHUNKS, ROWS, WIDE),
            vmem(CHUNKS, 8 * cap_y, WIDE),
            vmem(CHUNKS, 8 * cap_y, WIDE),
            vmem(CHUNKS, 8 * cap_z, WIDE),
            vmem(CHUNKS, 8 * cap_z, WIDE),
            vmem(BACKS, 8 * cap_z, BACK),
            vmem(BACKS, 8 * cap_z, BACK),
            vmem(BACKS, 8 * cap_y, BACK),
            vmem(BACKS, 8 * cap_y, BACK),
            vmem(BACKS, ROWS, BACK),
            vmem(2 * KH * PRE, D),
            vmem(2 * KH * PRE, D),
            vmem(2 * KH * PRE, D),
            vmem(8 * cap_y, ROWS),
            vmem(8 * cap_z, 8 * cap_y),
            vmem(ROWS, 8 * cap_z),
            vmem(ROWS, 8 * cap_y),
            vmem(8 * cap_y, 8 * cap_z),
            vmem(8 * cap_z, ROWS),
            vmem(ROWS, ROWS, dtype=F32),
            vmem(KH, 2, PRE, D, dtype=F32),
            vmem(KH, PRE, D, dtype=F32),
            vmem(KH, PRE, D, dtype=F32),
            vmem(KH, PRE, D, dtype=F32),
            vmem(KH, 2, PRE, D, dtype=F32),
            dma((3,)),
            dma((3,)),
            dma((CHUNKS,)),
            dma((CHUNKS,)),
            dma((CHUNKS,)),
            dma((CHUNKS,)),
            dma((CHUNKS,)),
            dma((CHUNKS,)),
            dma((BACKS,)),
            dma((BACKS,)),
            dma((BACKS,)),
            dma((BACKS,)),
            dma((BACKS,)),
            dma((BACKS,)),
            dma((3,)),
            dma((3,)),
            dma((KH, 3)),
            dma((KH, 4)),
        ],
        compiler_params=pltpu.CompilerParams(
            collective_id=0, has_side_effects=True, vmem_limit_bytes=60 * 2**20
        ),
    )(*operands)


def body(
    roll_query, roll_key, roll_value, roll_cotangent, route, arrival, lengths, prefix_kv, owner
):
    tp = lax.axis_index("tp")
    group = lax.axis_index("grp") // TP
    line = jnp.arange(ROWS, dtype=I32) // SEND
    routes = jnp.broadcast_to(jnp.where(line == tp, jnp.tile(route, TP), 0)[None], (8, ROWS))
    arrivals = jnp.broadcast_to(arrival[:, None], (ROWS, D))
    sizes = jnp.broadcast_to(
        jnp.concatenate([lengths[0], lengths[0]])[:, None].astype(I32), (8, D)
    )
    held = jnp.transpose(prefix_kv[0].reshape(PRE, 2, KH, D), (1, 2, 0, 3))
    held = held.reshape(2 * KH * PRE, D)
    holder = jnp.broadcast_to(owner[group], (8, D))
    operands = (
        roll_query,
        roll_key,
        roll_value,
        roll_cotangent,
        routes,
        arrivals,
        sizes,
        held,
        holder,
    )
    grad_query, grad_key, grad_value, grad_prefix = whole_step(64, 64, operands)
    grad_prefix = jnp.transpose(grad_prefix, (2, 0, 1, 3)).reshape(1, PRE, 2, KH * D)
    return grad_query, grad_key, grad_value, grad_prefix


def solution(mesh):
    return jax.shard_map(
        body,
        mesh=mesh,
        in_specs=(
            P(("grp", "tp"), None),
            P(("grp", "tp"), None),
            P(("grp", "tp"), None),
            P(("grp", "tp"), None),
            P(("grp", "tp")),
            P("grp"),
            P("grp", None),
            P("grp", None, None, "tp"),
            P(),
        ),
        out_specs=(
            P(("grp", "tp"), None),
            P(("grp", "tp"), None),
            P(("grp", "tp"), None),
            P("grp", None, None, "tp"),
        ),
        check_vma=False,
    )
```

```python
import functools
import math

import jax
import jax.numpy as jnp
from jax import lax
from jax.experimental import pallas as pl
from jax.experimental.pallas import tpu as pltpu
from jax.sharding import PartitionSpec as P

MESH = pl.DeviceIdType.MESH
D = 128
TP = 4
PLANE = 8
RATIO = 5
KH = 2
ROWS = 256
SEND = 64
PRE = 512
CHUNKS = 6
WIDE = 512
BACKS = 8
BACK = 256
PITCH = 128
NEGATIVE = -1e30
SCALE = 1.0 / math.sqrt(D)
F32 = jnp.float32
BF16 = jnp.bfloat16
I32 = jnp.int32
WIDTHS = (128, 256, 256, 256)


def iota(shape, dim):
    return lax.broadcasted_iota(I32, shape, dim)


def hot(match):
    return jnp.where(match, 1.0, 0.0).astype(BF16)


def dot(a, b):
    return jnp.dot(a, b, preferred_element_type=F32)


def dot_nt(a, b):
    return lax.dot_general(a, b, (((1,), (1,)), ((), ())), preferred_element_type=F32)


def place(kind, valid, lanes, limit):
    classes = iota((8, lanes), 0)
    member = (kind == classes) & valid
    before = hot(iota((lanes, lanes), 0) < iota((lanes, lanes), 1))
    count = dot(hot(member), before)
    rank = jnp.sum(jnp.where(member, count, 0.0), axis=0, keepdims=True).astype(I32)
    kind, valid = kind[0:1], valid[0:1]
    slot = jnp.where(valid & (rank < limit), kind * limit + rank, -1)
    table = jnp.where(valid & (rank < limit), kind * PITCH + rank, -1)
    over = jnp.max(jnp.where(valid & (rank >= limit), 1.0, 0.0), axis=1, keepdims=True)
    return slot, table, over


def tabulate(code, table, over, lanes):
    sub = iota((8, lanes), 0)
    high, low = code >> 7, code & 127
    parts = jnp.where(sub == 0, high, jnp.where(sub == 1, low, 0)).astype(F32).astype(BF16)
    spread = hot(iota((8 * PITCH, lanes), 0) == table)
    return jnp.where(iota((8, 8 * PITCH), 0) == 2, over, dot_nt(parts, spread))


def flagged(table):
    return jnp.max(table[2:3], axis=1, keepdims=True)


def compacted(table, limit):
    lanes = 8 * limit
    lane = iota((8 * PITCH, lanes), 1)
    target = lane
    for i in range(1, 8):
        target = target + jnp.where(lane >= i * limit, PITCH - limit, 0)
    pick = hot(iota((8 * PITCH, lanes), 0) == target)
    parts = dot(table.astype(BF16), pick)
    return (parts[0:1] * 128.0 + parts[1:2]).astype(I32)


def turned(matrix):
    n = matrix.shape[1]
    eye = hot(iota((n, n), 0) == iota((n, n), 1))
    return dot_nt(eye, matrix).astype(BF16)


def kernel(
    cap_y,
    cap_z,
    query,
    key,
    value,
    cotangent,
    route,
    arrival,
    lengths,
    prefix,
    holder,
    grad_query,
    grad_key,
    grad_value,
    grad_prefix,
    overflow,
    x_table,
    y_table_out,
    y_table_in,
    z_table_out,
    z_table_in,
    flag_out,
    flag_in,
    x_in,
    y_out,
    y_in,
    z_out,
    z_in,
    bz_out,
    bz_in,
    by_out,
    by_in,
    bx_out,
    pre_in,
    pre_now,
    pre_far,
    to_y,
    to_z,
    to_rows,
    from_y,
    from_z,
    from_rows,
    mask,
    acc,
    acc_in,
    chip,
    chip_in,
    total,
    t_send,
    t_recv,
    x_send,
    x_recv,
    y_send,
    y_recv,
    z_send,
    z_recv,
    bz_send,
    bz_recv,
    by_send,
    by_recv,
    bx_send,
    bx_recv,
    p_send,
    p_recv,
    a_send,
    a_recv,
):
    grp = lax.axis_index("grp")
    tp = lax.axis_index("tp")
    plane = grp // PLANE
    spot = lax.rem(grp, PLANE)
    core = lax.rem(spot, 2)
    side = lax.rem(spot // 2, 2)
    mate = grp + 1 - 2 * core
    across = grp + 2 - 4 * side

    def x_peer(k):
        return lax.rem(tp + k, TP)

    def y_peer(k):
        return lax.rem(spot + k, PLANE)

    def z_peer(k):
        return lax.rem(plane + k, PLANE)

    def at_x(k):
        return (grp, x_peer(k))

    def at_y(k):
        return (plane * PLANE + y_peer(k), tp)

    def at_z(k):
        return (z_peer(k) * PLANE + spot, tp)

    def block(index, size):
        return pl.ds(pl.multiple_of(index * size, size), size)

    def remote(src, dst, send, recv, device):
        copy = pltpu.make_async_remote_copy(
            src_ref=src,
            dst_ref=dst,
            send_sem=send,
            recv_sem=recv,
            device_id=device,
            device_id_type=MESH,
        )
        copy.start()
        return copy

    def local(src, dst, sem):
        pltpu.make_async_copy(src, dst, sem).start()

    def await_bytes(ref, sem):
        pltpu.make_async_copy(ref, ref, sem).wait()

    entry = pltpu.get_barrier_semaphore()
    for k in range(1, TP):
        pl.semaphore_signal(entry, inc=1, device_id=at_x(k), device_id_type=MESH)
    for k in range(1, PLANE):
        pl.semaphore_signal(entry, inc=1, device_id=at_y(k), device_id_type=MESH)
    for k in range(1, PLANE):
        pl.semaphore_signal(entry, inc=1, device_id=at_z(k), device_id_type=MESH)
    pl.semaphore_wait(entry, TP - 1 + 2 * (PLANE - 1))

    for k in range(1, TP):
        remote(route, x_table.at[k - 1], t_send.at[0], t_recv.at[0], at_x(k))

    def chunk_parts(chunk, to):
        kh, part = chunk // 3, chunk % 3
        head = to * (KH * RATIO) + kh * RATIO
        if part == 0:
            return (
                (key, to * KH + kh, 1),
                (value, to * KH + kh, 1),
                (query, head, 1),
                (cotangent, head, 1),
            )
        first = head + 2 * part - 1
        return ((query, first, 2), (cotangent, first, 2))

    def x_stage(chunk):
        for k in range(TP):
            to = x_peer(k)
            lane = 0
            for source, head, heads in chunk_parts(chunk, to):
                src = source.at[:, pl.ds(pl.multiple_of(head * D, D), heads * D)]
                dst = x_in.at[chunk, block(tp, SEND), pl.ds(lane, heads * D)]
                if k == 0:
                    local(src, dst, x_recv.at[chunk])
                else:
                    remote(src, dst, x_send.at[chunk], x_recv.at[chunk], at_x(k))
                lane += heads * D

    x_stage(0)
    remote(prefix, pre_in, p_send.at[0], p_recv.at[0], (mate, tp))
    for chunk in range(1, CHUNKS):
        x_stage(chunk)

    await_bytes(x_table, t_recv.at[0])
    routes = route[...] + x_table[0] + x_table[1] + x_table[2]
    trainer = routes >> 1
    line = iota((8, ROWS), 1) // SEND
    number = grp * (2 * TP) + line * 2 + (routes & 1)
    code = ((trainer >> 3) * 512 + number + 1)[0:1]
    slot, table, over = place(trainer & 7, trainer >= 0, ROWS, cap_y)
    to_y[...] = hot(iota((8 * cap_y, ROWS), 0) == slot)
    y_table_out[...] = tabulate(code, table, over, ROWS)
    for k in range(1, PLANE):
        remote(
            y_table_out.at[:, block(y_peer(k), PITCH)],
            y_table_in.at[:, block(spot, PITCH)],
            t_send.at[1],
            t_recv.at[1],
            at_y(k),
        )
    local(
        y_table_out.at[:, block(spot, PITCH)], y_table_in.at[:, block(spot, PITCH)], t_recv.at[1]
    )

    def y_stage(chunk):
        await_bytes(x_in.at[chunk], x_recv.at[chunk])
        y_out[chunk] = dot(to_y[...], x_in[chunk]).astype(BF16)
        for k in range(1, PLANE):
            remote(
                y_out.at[chunk, block(y_peer(k), cap_y)],
                y_in.at[chunk, block(spot, cap_y)],
                y_send.at[chunk],
                y_recv.at[chunk],
                at_y(k),
            )
        local(
            y_out.at[chunk, block(spot, cap_y)],
            y_in.at[chunk, block(spot, cap_y)],
            y_recv.at[chunk],
        )

    def z_stage(chunk):
        await_bytes(y_in.at[chunk], y_recv.at[chunk])
        z_out[chunk] = dot(to_z[...], y_in[chunk]).astype(BF16)
        for k in (4, 3, 5, 2, 6, 1, 7):
            remote(
                z_out.at[chunk, block(z_peer(k), cap_z)],
                z_in.at[chunk, block(plane, cap_z)],
                z_send.at[chunk],
                z_recv.at[chunk],
                at_z(k),
            )
        local(
            z_out.at[chunk, block(plane, cap_z)],
            z_in.at[chunk, block(plane, cap_z)],
            z_recv.at[chunk],
        )

    y_stage(0)
    y_stage(1)

    await_bytes(y_table_in, t_recv.at[1])
    code = compacted(y_table_in[...], cap_y)
    lanes = 8 * cap_y
    code8 = jnp.broadcast_to(code, (8, lanes))
    slot, table, over = place((code8 - 1) >> 9, code8 > 0, lanes, cap_z)
    to_z[...] = hot(iota((8 * cap_z, lanes), 0) == slot)
    over = jnp.maximum(over, flagged(y_table_in[...]))
    z_table_out[...] = tabulate(((code - 1) & 511) + 1, table, over, lanes)
    for k in range(1, PLANE):
        remote(
            z_table_out.at[:, block(z_peer(k), PITCH)],
            z_table_in.at[:, block(plane, PITCH)],
            t_send.at[2],
            t_recv.at[2],
            at_z(k),
        )
    local(
        z_table_out.at[:, block(plane, PITCH)], z_table_in.at[:, block(plane, PITCH)], t_recv.at[2]
    )

    z_stage(0)

    hold = holder[0:1, :]
    await_bytes(pre_in, p_recv.at[0])
    mine = (hold & 1) == core
    pre_now[...] = jnp.where(
        mine, prefix[...].astype(F32), pre_in[...].astype(F32)
    ).astype(BF16)
    remote(
        pre_now.at[block(core, 2 * PRE)],
        pre_far.at[block(core, 2 * PRE)],
        p_send.at[1],
        p_recv.at[1],
        (across, tp),
    )

    y_stage(2)
    z_stage(1)
    y_stage(3)
    z_stage(2)
    await_bytes(pre_far.at[block(core, 2 * PRE)], p_recv.at[1])
    remote(
        pre_far.at[block(core, 2 * PRE)],
        pre_far.at[block(core, 2 * PRE)],
        p_send.at[2],
        p_recv.at[2],
        (mate, tp),
    )
    y_stage(4)
    z_stage(3)
    y_stage(5)
    z_stage(4)
    z_stage(5)

    ends = [lengths[0:1, :]]
    for i in range(1, 3):
        ends.append(ends[-1] + lengths[i : i + 1, :])
    query_row = iota((ROWS, ROWS), 1)
    key_row = iota((ROWS, ROWS), 0)
    same = key_row <= query_row
    for end in ends:
        end = jnp.concatenate([end, end], axis=1)
        same = same & ((key_row >= end) == (query_row >= end))
    mask[...] = jnp.where(same, 0.0, NEGATIVE)
    await_bytes(pre_far.at[block(1 - core, 2 * PRE)], p_recv.at[2])
    await_bytes(pre_now.at[pl.ds(0, 2 * PRE)], p_send.at[1])
    here = (hold >> 1) == side
    pre_now[...] = jnp.where(
        here, pre_now[...].astype(F32), pre_far[...].astype(F32)
    ).astype(BF16)
    from_y[...] = turned(to_y[...])
    from_z[...] = turned(to_z[...])

    await_bytes(z_table_in, t_recv.at[2])
    code = compacted(z_table_in[...], cap_z) - 1
    flag_out[...] = jnp.broadcast_to(flagged(z_table_in[...]), (8, PITCH))
    for k in range(1, PLANE):
        remote(flag_out, flag_in.at[k - 1], t_send.at[3], t_recv.at[3], at_y(k))
    rows = hot(arrival[:, 0:1] == code)
    to_rows[...] = rows
    from_rows[...] = turned(rows)

    def back_z(chunk, result):
        wide = result.shape[1]
        lanes = pl.ds(0, wide)
        bz_out[chunk, :, 0:wide] = dot(from_rows[...], result).astype(BF16)
        for k in (4, 3, 5, 2, 6, 1, 7):
            remote(
                bz_out.at[chunk, block(z_peer(k), cap_z), lanes],
                bz_in.at[chunk, block(plane, cap_z), lanes],
                bz_send.at[chunk],
                bz_recv.at[chunk],
                at_z(k),
            )
        local(
            bz_out.at[chunk, block(plane, cap_z), lanes],
            bz_in.at[chunk, block(plane, cap_z), lanes],
            bz_recv.at[chunk],
        )

    def back_y(chunk):
        wide = WIDTHS[chunk % 4]
        lanes = pl.ds(0, wide)
        await_bytes(bz_in.at[chunk, :, lanes], bz_recv.at[chunk])
        by_out[chunk, :, 0:wide] = dot(from_z[...], bz_in[chunk, :, 0:wide]).astype(BF16)
        for k in range(1, PLANE):
            remote(
                by_out.at[chunk, block(y_peer(k), cap_y), lanes],
                by_in.at[chunk, block(spot, cap_y), lanes],
                by_send.at[chunk],
                by_recv.at[chunk],
                at_y(k),
            )
        local(
            by_out.at[chunk, block(spot, cap_y), lanes],
            by_in.at[chunk, block(spot, cap_y), lanes],
            by_recv.at[chunk],
        )

    def back_x(chunk):
        kh, part = chunk // 4, chunk % 4
        wide = WIDTHS[part]
        lanes = pl.ds(0, wide)
        await_bytes(by_in.at[chunk, :, lanes], by_recv.at[chunk])
        bx_out[chunk, :, 0:wide] = dot(from_y[...], by_in[chunk, :, 0:wide]).astype(BF16)
        head = tp * (KH * RATIO) + kh * RATIO
        if part < 3:
            first = head if part == 0 else head + 2 * part - 1
            parts = ((grad_query, first, wide // D),)
        else:
            parts = ((grad_key, tp * KH + kh, 1), (grad_value, tp * KH + kh, 1))
        for k in range(TP):
            lane = 0
            for target, head, heads in parts:
                src = bx_out.at[chunk, block(x_peer(k), SEND), pl.ds(lane, heads * D)]
                dst = target.at[:, pl.ds(pl.multiple_of(head * D, D), heads * D)]
                if k == 0:
                    local(src, dst, bx_recv.at[chunk])
                else:
                    remote(src, dst, bx_send.at[chunk], bx_recv.at[chunk], at_x(k))
                lane += heads * D

    def reduce_core(kh):
        remote(acc.at[kh, 1 - core], acc_in.at[kh], a_send.at[kh, 0], a_recv.at[kh, 0], (mate, tp))

    def reduce_side(kh):
        await_bytes(acc_in.at[kh], a_recv.at[kh, 0])
        chip[kh] = acc[kh, core] + acc_in[kh]
        remote(chip.at[kh], chip_in.at[kh], a_send.at[kh, 1], a_recv.at[kh, 1], (across, tp))

    def reduce_end(kh):
        await_bytes(chip_in.at[kh], a_recv.at[kh, 1])
        whole = chip[kh] + chip_in[kh]
        total[kh, 0] = jnp.where(hold == 2 * side + core, whole, 0.0)
        total[kh, 1] = jnp.where(hold == 2 * side + 1 - core, whole, 0.0)
        local(total.at[kh, 0], grad_prefix.at[core, kh], a_recv.at[kh, 2])
        remote(
            total.at[kh, 1], grad_prefix.at[core, kh], a_send.at[kh, 2], a_recv.at[kh, 3], (mate, tp)
        )

    def tokens(chunk):
        await_bytes(z_in.at[chunk], z_recv.at[chunk])
        return dot(to_rows[...], z_in[chunk]).astype(BF16)

    def attend(keys, values, keys_t, queries, grads, key_grad, value_grad):
        scores = dot_nt(keys, queries) * SCALE
        scores = jnp.concatenate([scores[:PRE], scores[PRE:] + mask[...]], axis=0)
        weights = jnp.exp(scores - jnp.max(scores, axis=0, keepdims=True))
        probability = weights * (1.0 / jnp.sum(weights, axis=0, keepdims=True))
        grad_prob = dot_nt(values, grads)
        delta = jnp.sum(probability * grad_prob, axis=0, keepdims=True)
        dscore = (probability * (grad_prob - delta)).astype(BF16)
        key_part = dot(dscore, queries)
        value_part = dot(probability.astype(BF16), grads)
        query_grad = (jnp.transpose(dot(keys_t, dscore)) * SCALE).astype(BF16)
        if key_grad is None:
            return query_grad, key_part, value_part
        return query_grad, key_grad + key_part, value_grad + value_part

    later = []
    for kh in range(KH):
        base = kh * 3
        got = tokens(base)
        lower = kh * PRE
        keys = jnp.concatenate([pre_now[lower : lower + PRE], got[:, 0:D]], axis=0)
        values = jnp.concatenate(
            [pre_now[KH * PRE + lower : KH * PRE + lower + PRE], got[:, D : 2 * D]], axis=0
        )
        keys_t = jnp.transpose(keys.astype(F32)).astype(BF16)
        key_grad = value_grad = None
        for part in range(3):
            if part == 0:
                pairs = ((got[:, 2 * D : 3 * D], got[:, 3 * D :]),)
            else:
                got = tokens(base + part)
                pairs = ((got[:, :D], got[:, 2 * D : 3 * D]), (got[:, D : 2 * D], got[:, 3 * D :]))
            results = []
            for queries, grads in pairs:
                result, key_grad, value_grad = attend(
                    keys, values, keys_t, queries, grads, key_grad, value_grad
                )
                results.append(result)
            whole = results[0] if part == 0 else jnp.concatenate(results, axis=1)
            back_z(kh * 4 + part, whole)
            if kh == 1:
                back_y(part)
                if part > 0:
                    back_x(part - 1)
        own = [(key_grad[PRE:] * SCALE).astype(BF16), value_grad[PRE:].astype(BF16)]
        back_z(kh * 4 + 3, jnp.concatenate(own, axis=1))
        acc[kh, 0] = key_grad[:PRE] * SCALE
        acc[kh, 1] = value_grad[:PRE]
        reduce_core(kh)
        if kh == 1:
            reduce_side(0)

    back_y(3)
    back_x(2)
    reduce_side(1)
    back_y(4)
    back_x(3)
    reduce_end(0)
    back_y(5)
    back_x(4)
    back_y(6)
    back_x(5)
    reduce_end(1)
    back_y(7)
    back_x(6)
    await_bytes(flag_in, t_recv.at[3])
    overflow[...] = jnp.maximum(flag_out[...], jnp.max(flag_in[...], axis=0))
    back_x(7)

    for i in range(TP - 1):
        await_bytes(route, t_send.at[0])
    await_bytes(flag_in, t_send.at[3])
    for i, ref in ((1, y_table_out), (2, z_table_out)):
        await_bytes(ref.at[:, pl.ds(0, 7 * PITCH)], t_send.at[i])
    for chunk in range(CHUNKS):
        await_bytes(x_in.at[chunk, pl.ds(0, 3 * SEND)], x_send.at[chunk])
        await_bytes(y_out.at[chunk, pl.ds(0, 7 * cap_y)], y_send.at[chunk])
        await_bytes(z_out.at[chunk, pl.ds(0, 7 * cap_z)], z_send.at[chunk])
    for chunk in range(BACKS):
        lanes = pl.ds(0, WIDTHS[chunk % 4])
        await_bytes(bz_out.at[chunk, pl.ds(0, 7 * cap_z), lanes], bz_send.at[chunk])
        await_bytes(by_out.at[chunk, pl.ds(0, 7 * cap_y), lanes], by_send.at[chunk])
        await_bytes(bx_out.at[chunk, pl.ds(0, 3 * SEND), lanes], bx_send.at[chunk])
        await_bytes(bx_out.at[chunk, :, lanes], bx_recv.at[chunk])
    await_bytes(prefix, p_send.at[0])
    await_bytes(pre_now.at[pl.ds(0, 2 * PRE)], p_send.at[2])
    for kh in range(KH):
        await_bytes(acc_in.at[kh], a_send.at[kh, 0])
        await_bytes(chip.at[kh], a_send.at[kh, 1])
        await_bytes(chip.at[kh], a_send.at[kh, 2])
        await_bytes(chip.at[kh], a_recv.at[kh, 2])
        await_bytes(chip.at[kh], a_recv.at[kh, 3])


def whole_step(cap_y, cap_z, number, operands):
    def vmem(*shape, dtype=BF16):
        return pltpu.VMEM(shape, dtype)

    dma = pltpu.SemaphoreType.DMA
    in_vmem = pl.BlockSpec(memory_space=pltpu.VMEM)
    anywhere = pl.BlockSpec(memory_space=pl.ANY)
    return pl.pallas_call(
        functools.partial(kernel, cap_y, cap_z),
        out_shape=(
            jax.ShapeDtypeStruct((SEND, TP * KH * RATIO * D), BF16),
            jax.ShapeDtypeStruct((SEND, TP * KH * D), BF16),
            jax.ShapeDtypeStruct((SEND, TP * KH * D), BF16),
            jax.ShapeDtypeStruct((2, KH, PRE, D), F32),
            jax.ShapeDtypeStruct((8, PITCH), F32),
        ),
        in_specs=[anywhere] * 4 + [in_vmem] * 5,
        out_specs=(anywhere,) * 4 + (in_vmem,),
        scratch_shapes=[
            vmem(TP - 1, 8, ROWS, dtype=I32),
            vmem(8, 8 * PITCH, dtype=F32),
            vmem(8, 8 * PITCH, dtype=F32),
            vmem(8, 8 * PITCH, dtype=F32),
            vmem(8, 8 * PITCH, dtype=F32),
            vmem(8, PITCH, dtype=F32),
            vmem(PLANE - 1, 8, PITCH, dtype=F32),
            vmem(CHUNKS, ROWS, WIDE),
            vmem(CHUNKS, 8 * cap_y, WIDE),
            vmem(CHUNKS, 8 * cap_y, WIDE),
            vmem(CHUNKS, 8 * cap_z, WIDE),
            vmem(CHUNKS, 8 * cap_z, WIDE),
            vmem(BACKS, 8 * cap_z, BACK),
            vmem(BACKS, 8 * cap_z, BACK),
            vmem(BACKS, 8 * cap_y, BACK),
            vmem(BACKS, 8 * cap_y, BACK),
            vmem(BACKS, ROWS, BACK),
            vmem(2 * KH * PRE, D),
            vmem(2 * KH * PRE, D),
            vmem(2 * KH * PRE, D),
            vmem(8 * cap_y, ROWS),
            vmem(8 * cap_z, 8 * cap_y),
            vmem(ROWS, 8 * cap_z),
            vmem(ROWS, 8 * cap_y),
            vmem(8 * cap_y, 8 * cap_z),
            vmem(8 * cap_z, ROWS),
            vmem(ROWS, ROWS, dtype=F32),
            vmem(KH, 2, PRE, D, dtype=F32),
            vmem(KH, PRE, D, dtype=F32),
            vmem(KH, PRE, D, dtype=F32),
            vmem(KH, PRE, D, dtype=F32),
            vmem(KH, 2, PRE, D, dtype=F32),
            dma((4,)),
            dma((4,)),
            dma((CHUNKS,)),
            dma((CHUNKS,)),
            dma((CHUNKS,)),
            dma((CHUNKS,)),
            dma((CHUNKS,)),
            dma((CHUNKS,)),
            dma((BACKS,)),
            dma((BACKS,)),
            dma((BACKS,)),
            dma((BACKS,)),
            dma((BACKS,)),
            dma((BACKS,)),
            dma((3,)),
            dma((3,)),
            dma((KH, 3)),
            dma((KH, 4)),
        ],
        compiler_params=pltpu.CompilerParams(
            collective_id=number, has_side_effects=True, vmem_limit_bytes=60 * 2**20
        ),
    )(*operands)


def body(
    roll_query, roll_key, roll_value, roll_cotangent, route, arrival, lengths, prefix_kv, owner
):
    tp = lax.axis_index("tp")
    group = lax.axis_index("grp") // TP
    line = jnp.arange(ROWS, dtype=I32) // SEND
    routes = jnp.broadcast_to(jnp.where(line == tp, jnp.tile(route, TP), 0)[None], (8, ROWS))
    arrivals = jnp.broadcast_to(arrival[:, None], (ROWS, D))
    sizes = jnp.broadcast_to(
        jnp.concatenate([lengths[0], lengths[0]])[:, None].astype(I32), (8, D)
    )
    held = jnp.transpose(prefix_kv[0].reshape(PRE, 2, KH, D), (1, 2, 0, 3))
    held = held.reshape(2 * KH * PRE, D)
    holder = jnp.broadcast_to(owner[group], (8, D))
    operands = (
        roll_query,
        roll_key,
        roll_value,
        roll_cotangent,
        routes,
        arrivals,
        sizes,
        held,
        holder,
    )
    *quick, overflow = whole_step(48, 48, 0, operands)
    grad_query, grad_key, grad_value, grad_prefix = lax.cond(
        overflow[0, 0] > 0.5,
        lambda: tuple(whole_step(64, 64, 1, operands)[:4]),
        lambda: tuple(quick),
    )
    grad_prefix = jnp.transpose(grad_prefix, (2, 0, 1, 3)).reshape(1, PRE, 2, KH * D)
    return grad_query, grad_key, grad_value, grad_prefix


def solution(mesh):
    return jax.shard_map(
        body,
        mesh=mesh,
        in_specs=(
            P(("grp", "tp"), None),
            P(("grp", "tp"), None),
            P(("grp", "tp"), None),
            P(("grp", "tp"), None),
            P(("grp", "tp")),
            P("grp"),
            P("grp", None),
            P("grp", None, None, "tp"),
            P(),
        ),
        out_specs=(
            P(("grp", "tp"), None),
            P(("grp", "tp"), None),
            P(("grp", "tp"), None),
            P("grp", None, None, "tp"),
        ),
        check_vma=False,
    )
```

```python
import functools
import math

import jax
import jax.numpy as jnp
from jax import lax
from jax.experimental import pallas as pl
from jax.experimental.pallas import tpu as pltpu
from jax.sharding import PartitionSpec as P

MESH = pl.DeviceIdType.MESH
D = 128
TP = 4
PLANE = 8
RATIO = 5
KH = 2
ROWS = 256
SEND = 64
PRE = 512
FORWARD = (
    (("k", 0, 1), ("v", 0, 1)),
    (("q", 0, 1), ("c", 0, 1)),
    (("q", 1, 2), ("c", 1, 2)),
    (("q", 3, 2), ("c", 3, 2)),
    (("k", 1, 1), ("v", 1, 1), ("q", 5, 1), ("c", 5, 1)),
    (("q", 6, 2), ("c", 6, 2)),
    (("q", 8, 1), ("c", 8, 1)),
    (("q", 9, 1), ("c", 9, 1)),
)
BACKWARD = (
    (("q", 0, 1),),
    (("q", 1, 2),),
    (("q", 3, 2),),
    (("k", 0, 1), ("v", 0, 1)),
    (("q", 5, 1),),
    (("q", 6, 2),),
    (("q", 8, 1),),
    (("q", 9, 1),),
    (("k", 1, 1), ("v", 1, 1)),
)
CHUNKS = len(FORWARD)
BACKS = len(BACKWARD)
WIDE = 512
BACK = 256
PITCH = 128
NEGATIVE = -1e30
SCALE = 1.0 / math.sqrt(D)
F32 = jnp.float32
BF16 = jnp.bfloat16
I32 = jnp.int32
AHEAD = 2
PROMPT = 5


def width(chunk):
    return D * sum(heads for _, _, heads in chunk)


def found(chunks, kind, head):
    for number, chunk in enumerate(chunks):
        lane = 0
        for name, first, heads in chunk:
            if name == kind and first <= head < first + heads:
                return number, lane + (head - first) * D
            lane += heads * D


def iota(shape, dim):
    return lax.broadcasted_iota(I32, shape, dim)


def hot(match):
    return jnp.where(match, 1.0, 0.0).astype(BF16)


def dot(a, b):
    return jnp.dot(a, b, preferred_element_type=F32)


def dot_nt(a, b):
    return lax.dot_general(a, b, (((1,), (1,)), ((), ())), preferred_element_type=F32)


def place(kind, valid, lanes, limit):
    classes = iota((8, lanes), 0)
    member = (kind == classes) & valid
    before = hot(iota((lanes, lanes), 0) < iota((lanes, lanes), 1))
    count = dot(hot(member), before)
    rank = jnp.sum(jnp.where(member, count, 0.0), axis=0, keepdims=True).astype(I32)
    kind, valid = kind[0:1], valid[0:1]
    slot = jnp.where(valid & (rank < limit), kind * limit + rank, -1)
    table = jnp.where(valid & (rank < limit), kind * PITCH + rank, -1)
    over = jnp.max(jnp.where(valid & (rank >= limit), 1.0, 0.0), axis=1, keepdims=True)
    return slot, table, over


def tabulate(code, table, over, lanes):
    sub = iota((8, lanes), 0)
    high, low = code >> 7, code & 127
    parts = jnp.where(sub == 0, high, jnp.where(sub == 1, low, 0)).astype(F32).astype(BF16)
    spread = hot(iota((8 * PITCH, lanes), 0) == table)
    return jnp.where(iota((8, 8 * PITCH), 0) == 2, over, dot_nt(parts, spread))


def flagged(table):
    return jnp.max(table[2:3], axis=1, keepdims=True)


def compacted(table, limit, column=False):
    lanes = 8 * limit
    lane = iota((8 * PITCH, lanes), 1)
    target = lane
    for i in range(1, 8):
        target = target + jnp.where(lane >= i * limit, PITCH - limit, 0)
    pick = hot(iota((8 * PITCH, lanes), 0) == target)
    if column:
        parts = lax.dot_general(
            pick, table.astype(BF16), (((0,), (1,)), ((), ())), preferred_element_type=F32
        )
        return (parts[:, 0:1] * 128.0 + parts[:, 1:2]).astype(I32)
    parts = dot(table.astype(BF16), pick)
    return (parts[0:1] * 128.0 + parts[1:2]).astype(I32)


def turned(matrix):
    n = matrix.shape[1]
    eye = hot(iota((n, n), 0) == iota((n, n), 1))
    return dot_nt(eye, matrix).astype(BF16)


def kernel(
    cap_y,
    cap_z,
    query,
    key,
    value,
    cotangent,
    route,
    arrival,
    lengths,
    prefix,
    owner,
    grad_query,
    grad_key,
    grad_value,
    grad_prefix,
    overflow,
    x_table_out,
    x_table,
    y_table_out,
    y_table_in,
    z_table_out,
    z_table_in,
    flag_out,
    flag_in,
    x_in,
    y_out,
    y_in,
    z_out,
    z_in,
    bz_out,
    bz_in,
    by_out,
    by_in,
    bx_out,
    pre_raw,
    pre_own,
    pre_in,
    pre_now,
    pre_far,
    to_y,
    to_z,
    to_rows,
    from_y,
    from_z,
    from_rows,
    mask,
    acc,
    acc_in,
    chip,
    chip_in,
    total,
    total_in,
    t_send,
    t_recv,
    x_send,
    x_recv,
    y_send,
    y_recv,
    z_send,
    z_recv,
    bz_send,
    bz_recv,
    by_send,
    by_recv,
    bx_send,
    bx_recv,
    p_send,
    p_recv,
    a_send,
    a_recv,
):
    grp = lax.axis_index("grp")
    tp = lax.axis_index("tp")
    plane = grp // PLANE
    spot = lax.rem(grp, PLANE)
    core = lax.rem(spot, 2)
    side = lax.rem(spot // 2, 2)
    mate = grp + 1 - 2 * core
    across = grp + 2 - 4 * side

    def x_peer(k):
        return lax.rem(tp + k, TP)

    def y_peer(k):
        return lax.rem(spot + k, PLANE)

    def z_peer(k):
        return lax.rem(plane + k, PLANE)

    def at_x(k):
        return (grp, x_peer(k))

    def at_y(k):
        return (plane * PLANE + y_peer(k), tp)

    def at_z(k):
        return (z_peer(k) * PLANE + spot, tp)

    def block(index, size):
        return pl.ds(pl.multiple_of(index * size, size), size)

    def remote(src, dst, send, recv, device):
        copy = pltpu.make_async_remote_copy(
            src_ref=src,
            dst_ref=dst,
            send_sem=send,
            recv_sem=recv,
            device_id=device,
            device_id_type=MESH,
        )
        copy.start()
        return copy

    def local(src, dst, sem):
        pltpu.make_async_copy(src, dst, sem).start()

    def await_bytes(ref, sem):
        pltpu.make_async_copy(ref, ref, sem).wait()

    local(prefix.at[0], pre_raw, p_recv.at[3])
    entry = pltpu.get_barrier_semaphore()
    for k in range(1, TP):
        pl.semaphore_signal(entry, inc=1, device_id=at_x(k), device_id_type=MESH)
    for k in range(1, PLANE):
        pl.semaphore_signal(entry, inc=1, device_id=at_y(k), device_id_type=MESH)
    for k in range(1, PLANE):
        pl.semaphore_signal(entry, inc=1, device_id=at_z(k), device_id_type=MESH)
    pl.semaphore_wait(entry, TP - 1 + 2 * (PLANE - 1))

    x_table_out[...] = jnp.broadcast_to(route[...].reshape(1, SEND), (8, SEND)).astype(F32)
    for k in range(1, TP):
        remote(x_table_out, x_table.at[k - 1], t_send.at[0], t_recv.at[0], at_x(k))

    def place_of(kind, head, device):
        per = KH if kind in "kv" else KH * RATIO
        return pl.multiple_of((device * per + head) * D, D)

    def x_stage(chunk):
        if chunk >= CHUNKS:
            return
        sources = {"q": query, "k": key, "v": value, "c": cotangent}
        for k in range(TP):
            to = x_peer(k)
            lane = 0
            for kind, head, heads in FORWARD[chunk]:
                src = sources[kind].at[:, pl.ds(place_of(kind, head, to), heads * D)]
                dst = x_in.at[chunk, block(tp, SEND), pl.ds(lane, heads * D)]
                if k == 0:
                    local(src, dst, x_recv.at[chunk])
                else:
                    remote(src, dst, x_send.at[chunk], x_recv.at[chunk], at_x(k))
                lane += heads * D

    for chunk in range(AHEAD):
        x_stage(chunk)

    await_bytes(pre_raw, p_recv.at[3])
    for kv in range(2):
        part = pre_raw[:, kv, :]
        for kh in range(KH):
            lower = (kv * KH + kh) * PRE
            pre_own[lower : lower + PRE] = part[:, kh * D : (kh + 1) * D]
    remote(pre_own, pre_in, p_send.at[0], p_recv.at[0], (mate, tp))

    await_bytes(x_table, t_recv.at[0])
    routes = jnp.zeros((8, ROWS), F32)
    for k in range(TP):
        begin = lax.rem(tp + TP - k, TP) * SEND
        spread = hot(iota((SEND, ROWS), 0) + begin == iota((SEND, ROWS), 1))
        heard = x_table_out[...] if k == 0 else x_table[k - 1]
        routes = routes + dot(heard.astype(BF16), spread)
    routes = routes.astype(I32)
    trainer = routes >> 1
    line = iota((8, ROWS), 1) // SEND
    number = grp * (2 * TP) + line * 2 + (routes & 1)
    code = ((trainer >> 3) * 512 + number + 1)[0:1]
    slot, table, over = place(trainer & 7, trainer >= 0, ROWS, cap_y)
    to_y[...] = hot(iota((8 * cap_y, ROWS), 0) == slot)
    y_table_out[...] = tabulate(code, table, over, ROWS)
    for k in range(1, PLANE):
        remote(
            y_table_out.at[:, block(y_peer(k), PITCH)],
            y_table_in.at[:, block(spot, PITCH)],
            t_send.at[1],
            t_recv.at[1],
            at_y(k),
        )
    local(
        y_table_out.at[:, block(spot, PITCH)], y_table_in.at[:, block(spot, PITCH)], t_recv.at[1]
    )

    def y_stage(chunk):
        wide = width(FORWARD[chunk])
        lanes = pl.ds(0, wide)
        await_bytes(x_in.at[chunk, :, lanes], x_recv.at[chunk])
        x_stage(chunk + AHEAD)
        y_out[chunk, :, 0:wide] = dot(to_y[...], x_in[chunk, :, 0:wide]).astype(BF16)
        for k in range(1, PLANE):
            remote(
                y_out.at[chunk, block(y_peer(k), cap_y), lanes],
                y_in.at[chunk, block(spot, cap_y), lanes],
                y_send.at[chunk],
                y_recv.at[chunk],
                at_y(k),
            )
        local(
            y_out.at[chunk, block(spot, cap_y), lanes],
            y_in.at[chunk, block(spot, cap_y), lanes],
            y_recv.at[chunk],
        )

    def z_stage(chunk):
        wide = width(FORWARD[chunk])
        lanes = pl.ds(0, wide)
        await_bytes(y_in.at[chunk, :, lanes], y_recv.at[chunk])
        z_out[chunk, :, 0:wide] = dot(to_z[...], y_in[chunk, :, 0:wide]).astype(BF16)
        for k in (4, 3, 5, 2, 6, 1, 7):
            remote(
                z_out.at[chunk, block(z_peer(k), cap_z), lanes],
                z_in.at[chunk, block(plane, cap_z), lanes],
                z_send.at[chunk],
                z_recv.at[chunk],
                at_z(k),
            )
        local(
            z_out.at[chunk, block(plane, cap_z), lanes],
            z_in.at[chunk, block(plane, cap_z), lanes],
            z_recv.at[chunk],
        )

    y_stage(0)
    y_stage(1)

    await_bytes(y_table_in, t_recv.at[1])
    code = compacted(y_table_in[...], cap_y)
    lanes = 8 * cap_y
    code8 = jnp.broadcast_to(code, (8, lanes))
    slot, table, over = place((code8 - 1) >> 9, code8 > 0, lanes, cap_z)
    to_z[...] = hot(iota((8 * cap_z, lanes), 0) == slot)
    over = jnp.maximum(over, flagged(y_table_in[...]))
    z_table_out[...] = tabulate(((code - 1) & 511) + 1, table, over, lanes)
    for k in range(1, PLANE):
        remote(
            z_table_out.at[:, block(z_peer(k), PITCH)],
            z_table_in.at[:, block(plane, PITCH)],
            t_send.at[2],
            t_recv.at[2],
            at_z(k),
        )
    local(
        z_table_out.at[:, block(plane, PITCH)], z_table_in.at[:, block(plane, PITCH)], t_recv.at[2]
    )

    z_stage(0)

    hold = owner[grp // TP]

    def prompt_across():
        await_bytes(pre_in, p_recv.at[0])
        mine = (hold & 1) == core
        pre_now[...] = jnp.where(mine, pre_own[...].astype(F32), pre_in[...].astype(F32)).astype(BF16)
        remote(
            pre_now.at[block(core, 2 * PRE)],
            pre_far.at[block(core, 2 * PRE)],
            p_send.at[1],
            p_recv.at[1],
            (across, tp),
        )

    def prompt_mate():
        await_bytes(pre_far.at[block(core, 2 * PRE)], p_recv.at[1])
        remote(
            pre_far.at[block(core, 2 * PRE)],
            pre_far.at[block(core, 2 * PRE)],
            p_send.at[2],
            p_recv.at[2],
            (mate, tp),
        )

    for chunk in range(2, CHUNKS):
        y_stage(chunk)
        z_stage(chunk - 1)
        if chunk == PROMPT:
            prompt_across()
    z_stage(CHUNKS - 1)
    prompt_mate()

    query_row = iota((ROWS, ROWS), 1)
    key_row = iota((ROWS, ROWS), 0)
    same = key_row <= query_row
    end = 0
    for i in range(3):
        end = end + lengths[0, i]
        same = same & ((key_row >= end) == (query_row >= end))
    mask[...] = jnp.where(same, 0.0, NEGATIVE)
    await_bytes(pre_far.at[block(1 - core, 2 * PRE)], p_recv.at[2])
    await_bytes(pre_now.at[pl.ds(0, 2 * PRE)], p_send.at[1])
    here = (hold >> 1) == side
    pre_now[...] = jnp.where(here, pre_now[...].astype(F32), pre_far[...].astype(F32)).astype(BF16)
    from_y[...] = turned(to_y[...])
    from_z[...] = turned(to_z[...])

    await_bytes(z_table_in, t_recv.at[2])
    flag_out[...] = jnp.broadcast_to(flagged(z_table_in[...]), (8, PITCH))
    for k in range(1, PLANE):
        remote(flag_out, flag_in.at[k - 1], t_send.at[3], t_recv.at[3], at_y(k))
    code = compacted(z_table_in[...], cap_z, column=True) - 1
    rows = hot(code == arrival[...].reshape(1, ROWS))
    from_rows[...] = rows
    to_rows[...] = turned(rows)

    def back_z(chunk, result):
        wide = result.shape[1]
        lanes = pl.ds(0, wide)
        bz_out[chunk, :, 0:wide] = dot(from_rows[...], result).astype(BF16)
        for k in (4, 3, 5, 2, 6, 1, 7):
            remote(
                bz_out.at[chunk, block(z_peer(k), cap_z), lanes],
                bz_in.at[chunk, block(plane, cap_z), lanes],
                bz_send.at[chunk],
                bz_recv.at[chunk],
                at_z(k),
            )
        local(
            bz_out.at[chunk, block(plane, cap_z), lanes],
            bz_in.at[chunk, block(plane, cap_z), lanes],
            bz_recv.at[chunk],
        )

    def back_y(chunk):
        wide = width(BACKWARD[chunk])
        lanes = pl.ds(0, wide)
        await_bytes(bz_in.at[chunk, :, lanes], bz_recv.at[chunk])
        by_out[chunk, :, 0:wide] = dot(from_z[...], bz_in[chunk, :, 0:wide]).astype(BF16)
        for k in range(1, PLANE):
            remote(
                by_out.at[chunk, block(y_peer(k), cap_y), lanes],
                by_in.at[chunk, block(spot, cap_y), lanes],
                by_send.at[chunk],
                by_recv.at[chunk],
                at_y(k),
            )
        local(
            by_out.at[chunk, block(spot, cap_y), lanes],
            by_in.at[chunk, block(spot, cap_y), lanes],
            by_recv.at[chunk],
        )

    def back_x(chunk):
        wide = width(BACKWARD[chunk])
        lanes = pl.ds(0, wide)
        await_bytes(by_in.at[chunk, :, lanes], by_recv.at[chunk])
        bx_out[chunk, :, 0:wide] = dot(from_y[...], by_in[chunk, :, 0:wide]).astype(BF16)
        targets = {"q": grad_query, "k": grad_key, "v": grad_value}
        for k in range(TP):
            lane = 0
            for kind, head, heads in BACKWARD[chunk]:
                src = bx_out.at[chunk, block(x_peer(k), SEND), pl.ds(lane, heads * D)]
                dst = targets[kind].at[:, pl.ds(place_of(kind, head, tp), heads * D)]
                if k == 0:
                    local(src, dst, bx_recv.at[chunk])
                else:
                    remote(src, dst, bx_send.at[chunk], bx_recv.at[chunk], at_x(k))
                lane += heads * D

    def reduce_core(kh):
        remote(acc.at[kh, 1 - core], acc_in.at[kh], a_send.at[kh, 0], a_recv.at[kh, 0], (mate, tp))

    def reduce_side(kh):
        await_bytes(acc_in.at[kh], a_recv.at[kh, 0])
        chip[kh] = acc[kh, core] + acc_in[kh]
        remote(chip.at[kh], chip_in.at[kh], a_send.at[kh, 1], a_recv.at[kh, 1], (across, tp))

    def reduce_mate(kh):
        await_bytes(chip_in.at[kh], a_recv.at[kh, 1])
        total[kh] = chip[kh] + chip_in[kh]
        remote(total.at[kh], total_in.at[kh], a_send.at[kh, 2], a_recv.at[kh, 2], (mate, tp))

    def reduce_end(kh):
        await_bytes(total_in.at[kh], a_recv.at[kh, 2])
        mine, theirs = total[kh], total_in[kh]
        for kv in range(2):
            whole = jnp.where(core == kv, mine, theirs)
            whole = jnp.where(hold == 2 * side + core, whole, 0.0)
            grad_prefix[0, :, kv, kh * D : (kh + 1) * D] = whole

    def tokens(chunk):
        wide = width(FORWARD[chunk])
        await_bytes(z_in.at[chunk, :, pl.ds(0, wide)], z_recv.at[chunk])
        return dot(to_rows[...], z_in[chunk, :, 0:wide]).astype(BF16)

    def attend(keys, values, keys_t, queries, grads, key_grad, value_grad):
        scores = dot_nt(keys, queries) * SCALE
        scores = jnp.concatenate([scores[:PRE], scores[PRE:] + mask[...]], axis=0)
        weights = jnp.exp(scores - jnp.max(scores, axis=0, keepdims=True))
        probability = weights * (1.0 / jnp.sum(weights, axis=0, keepdims=True))
        grad_prob = dot_nt(values, grads)
        delta = jnp.sum(probability * grad_prob, axis=0, keepdims=True)
        dscore = (probability * (grad_prob - delta)).astype(BF16)
        key_part = dot(dscore, queries)
        value_part = dot(probability.astype(BF16), grads)
        query_grad = (jnp.transpose(dot(keys_t, dscore)) * SCALE).astype(BF16)
        if key_grad is None:
            return query_grad, key_part, value_part
        return query_grad, key_grad + key_part, value_grad + value_part

    arrived = {}

    def rows_of(kind, head):
        chunk, lane = found(FORWARD, kind, head)
        if chunk not in arrived:
            arrived[chunk] = tokens(chunk)
        return arrived[chunk][:, lane : lane + D]

    done = {}

    def finish(kind, head, value):
        done[kind, head] = value
        chunk, _ = found(BACKWARD, kind, head)
        names = [(k, h) for k, first, heads in BACKWARD[chunk] for h in range(first, first + heads)]
        if all(name in done for name in names):
            parts = [done[name] for name in names]
            back_z(chunk, parts[0] if len(parts) == 1 else jnp.concatenate(parts, axis=1))

    for kh in range(KH):
        lower = kh * PRE
        keys = jnp.concatenate([pre_now[lower : lower + PRE], rows_of("k", kh)], axis=0)
        values = jnp.concatenate(
            [pre_now[KH * PRE + lower : KH * PRE + lower + PRE], rows_of("v", kh)], axis=0
        )
        keys_t = jnp.transpose(keys.astype(F32)).astype(BF16)
        key_grad = value_grad = None
        for head in range(kh * RATIO, (kh + 1) * RATIO):
            result, key_grad, value_grad = attend(
                keys,
                values,
                keys_t,
                rows_of("q", head),
                rows_of("c", head),
                key_grad,
                value_grad,
            )
            finish("q", head, result)
        acc[kh, 0] = key_grad[:PRE] * SCALE
        acc[kh, 1] = value_grad[:PRE]
        reduce_core(kh)
        finish("k", kh, (key_grad[PRE:] * SCALE).astype(BF16))
        finish("v", kh, value_grad[PRE:].astype(BF16))
        if kh == 1:
            reduce_side(0)

    back_y(0)
    back_y(1)
    back_x(0)
    reduce_side(1)
    reduce_mate(0)
    for chunk in range(2, BACKS):
        back_y(chunk)
        back_x(chunk - 1)
        if chunk == 4:
            reduce_mate(1)
        if chunk == 5:
            reduce_end(0)
    reduce_end(1)
    await_bytes(flag_in, t_recv.at[3])
    overflow[0] = jnp.max(jnp.maximum(flag_out[...], jnp.max(flag_in[...], axis=0))).astype(I32)
    back_x(BACKS - 1)

    await_bytes(x_table, t_send.at[0])
    await_bytes(flag_in, t_send.at[3])
    for i, ref in ((1, y_table_out), (2, z_table_out)):
        await_bytes(ref.at[:, pl.ds(0, 7 * PITCH)], t_send.at[i])
    for chunk in range(CHUNKS):
        lanes = pl.ds(0, width(FORWARD[chunk]))
        await_bytes(x_in.at[chunk, pl.ds(0, 3 * SEND), lanes], x_send.at[chunk])
        await_bytes(y_out.at[chunk, pl.ds(0, 7 * cap_y), lanes], y_send.at[chunk])
        await_bytes(z_out.at[chunk, pl.ds(0, 7 * cap_z), lanes], z_send.at[chunk])
    for chunk in range(BACKS):
        lanes = pl.ds(0, width(BACKWARD[chunk]))
        await_bytes(bz_out.at[chunk, pl.ds(0, 7 * cap_z), lanes], bz_send.at[chunk])
        await_bytes(by_out.at[chunk, pl.ds(0, 7 * cap_y), lanes], by_send.at[chunk])
        await_bytes(bx_out.at[chunk, pl.ds(0, 3 * SEND), lanes], bx_send.at[chunk])
        await_bytes(bx_out.at[chunk, :, lanes], bx_recv.at[chunk])
    await_bytes(pre_own, p_send.at[0])
    await_bytes(pre_now.at[pl.ds(0, 2 * PRE)], p_send.at[2])
    for kh in range(KH):
        for i in range(3):
            await_bytes(chip.at[kh], a_send.at[kh, i])


def whole_step(cap_y, cap_z, number, operands):
    def vmem(*shape, dtype=BF16):
        return pltpu.VMEM(shape, dtype)

    dma = pltpu.SemaphoreType.DMA
    in_vmem = pl.BlockSpec(memory_space=pltpu.VMEM)
    in_smem = pl.BlockSpec(memory_space=pltpu.SMEM)
    anywhere = pl.BlockSpec(memory_space=pl.ANY)
    return pl.pallas_call(
        functools.partial(kernel, cap_y, cap_z),
        out_shape=(
            jax.ShapeDtypeStruct((SEND, TP * KH * RATIO * D), BF16),
            jax.ShapeDtypeStruct((SEND, TP * KH * D), BF16),
            jax.ShapeDtypeStruct((SEND, TP * KH * D), BF16),
            jax.ShapeDtypeStruct((1, PRE, 2, KH * D), F32),
            jax.ShapeDtypeStruct((1,), I32),
        ),
        in_specs=[anywhere] * 4 + [in_vmem] * 2 + [in_smem, anywhere, in_smem],
        out_specs=(anywhere,) * 3 + (in_vmem, in_smem),
        scratch_shapes=[
            vmem(8, SEND, dtype=F32),
            vmem(TP - 1, 8, SEND, dtype=F32),
            vmem(8, 8 * PITCH, dtype=F32),
            vmem(8, 8 * PITCH, dtype=F32),
            vmem(8, 8 * PITCH, dtype=F32),
            vmem(8, 8 * PITCH, dtype=F32),
            vmem(8, PITCH, dtype=F32),
            vmem(PLANE - 1, 8, PITCH, dtype=F32),
            vmem(CHUNKS, ROWS, WIDE),
            vmem(CHUNKS, 8 * cap_y, WIDE),
            vmem(CHUNKS, 8 * cap_y, WIDE),
            vmem(CHUNKS, 8 * cap_z, WIDE),
            vmem(CHUNKS, 8 * cap_z, WIDE),
            vmem(BACKS, 8 * cap_z, BACK),
            vmem(BACKS, 8 * cap_z, BACK),
            vmem(BACKS, 8 * cap_y, BACK),
            vmem(BACKS, 8 * cap_y, BACK),
            vmem(BACKS, ROWS, BACK),
            vmem(PRE, 2, KH * D),
            vmem(2 * KH * PRE, D),
            vmem(2 * KH * PRE, D),
            vmem(2 * KH * PRE, D),
            vmem(2 * KH * PRE, D),
            vmem(8 * cap_y, ROWS),
            vmem(8 * cap_z, 8 * cap_y),
            vmem(ROWS, 8 * cap_z),
            vmem(ROWS, 8 * cap_y),
            vmem(8 * cap_y, 8 * cap_z),
            vmem(8 * cap_z, ROWS),
            vmem(ROWS, ROWS, dtype=F32),
            vmem(KH, 2, PRE, D, dtype=F32),
            vmem(KH, PRE, D, dtype=F32),
            vmem(KH, PRE, D, dtype=F32),
            vmem(KH, PRE, D, dtype=F32),
            vmem(KH, PRE, D, dtype=F32),
            vmem(KH, PRE, D, dtype=F32),
            dma((4,)),
            dma((4,)),
            dma((CHUNKS,)),
            dma((CHUNKS,)),
            dma((CHUNKS,)),
            dma((CHUNKS,)),
            dma((CHUNKS,)),
            dma((CHUNKS,)),
            dma((BACKS,)),
            dma((BACKS,)),
            dma((BACKS,)),
            dma((BACKS,)),
            dma((BACKS,)),
            dma((BACKS,)),
            dma((3,)),
            dma((4,)),
            dma((KH, 3)),
            dma((KH, 3)),
        ],
        compiler_params=pltpu.CompilerParams(
            collective_id=number, has_side_effects=True, vmem_limit_bytes=60 * 2**20
        ),
    )(*operands)


def hand_out(*refs):
    sources, targets, sem = refs[:4], refs[4:8], refs[8]
    copies = [
        pltpu.make_async_copy(source, target, sem.at[i])
        for i, (source, target) in enumerate(zip(sources, targets))
    ]
    for copy in copies:
        copy.start()
    for copy in copies:
        copy.wait()


def handed_out(results):
    anywhere = pl.BlockSpec(memory_space=pl.ANY)
    return pl.pallas_call(
        hand_out,
        out_shape=tuple(jax.ShapeDtypeStruct(x.shape, x.dtype) for x in results),
        in_specs=[anywhere] * 4,
        out_specs=(anywhere,) * 4,
        scratch_shapes=[pltpu.SemaphoreType.DMA((4,))],
    )(*results)


def body(
    roll_query, roll_key, roll_value, roll_cotangent, route, arrival, lengths, prefix_kv, owner
):
    operands = (
        roll_query,
        roll_key,
        roll_value,
        roll_cotangent,
        route,
        arrival,
        lengths,
        prefix_kv,
        owner,
    )
    *quick, overflow = whole_step(48, 48, 0, operands)
    results = lax.cond(
        overflow[0] > 0,
        lambda: tuple(whole_step(64, 64, 1, operands)[:4]),
        lambda: tuple(quick),
    )
    return handed_out(results)


def solution(mesh):
    return jax.shard_map(
        body,
        mesh=mesh,
        in_specs=(
            P(("grp", "tp"), None),
            P(("grp", "tp"), None),
            P(("grp", "tp"), None),
            P(("grp", "tp"), None),
            P(("grp", "tp")),
            P("grp"),
            P("grp", None),
            P("grp", None, None, "tp"),
            P(),
        ),
        out_specs=(
            P(("grp", "tp"), None),
            P(("grp", "tp"), None),
            P(("grp", "tp"), None),
            P("grp", None, None, "tp"),
        ),
        check_vma=False,
    )
```

```python
import functools
import math

import jax
import jax.numpy as jnp
from jax import lax
from jax.experimental import pallas as pl
from jax.experimental.pallas import tpu as pltpu
from jax.sharding import PartitionSpec as P

MESH = pl.DeviceIdType.MESH
D = 128
TP = 4
PLANE = 8
RATIO = 5
KH = 2
ROWS = 256
SEND = 64
PRE = 512
FORWARD = (
    (("k", 0, 1),),
    (("v", 0, 1), ("q", 0, 1)),
    (("c", 0, 1),),
    (("q", 1, 2), ("c", 1, 2)),
    (("q", 3, 2), ("c", 3, 2)),
    (("k", 1, 1), ("v", 1, 1), ("q", 5, 1), ("c", 5, 1)),
    (("q", 6, 2), ("c", 6, 2)),
    (("q", 8, 1), ("c", 8, 1)),
    (("q", 9, 1), ("c", 9, 1)),
)
BACKWARD = (
    (("q", 0, 1),),
    (("q", 1, 2),),
    (("q", 3, 2),),
    (("k", 0, 1), ("v", 0, 1)),
    (("q", 5, 1),),
    (("q", 6, 2),),
    (("q", 8, 1),),
    (("q", 9, 1),),
    (("k", 1, 1),),
    (("v", 1, 1),),
)
CHUNKS = len(FORWARD)
BACKS = len(BACKWARD)
WIDE = 512
BACK = 256
PITCH = 128
NEGATIVE = -1e30
SCALE = 1.0 / math.sqrt(D)
F32 = jnp.float32
BF16 = jnp.bfloat16
I32 = jnp.int32
AHEAD = 2
PROMPT = 5


def width(chunk):
    return D * sum(heads for _, _, heads in chunk)


def found(chunks, kind, head):
    for number, chunk in enumerate(chunks):
        lane = 0
        for name, first, heads in chunk:
            if name == kind and first <= head < first + heads:
                return number, lane + (head - first) * D
            lane += heads * D


def iota(shape, dim):
    return lax.broadcasted_iota(I32, shape, dim)


def hot(match):
    return jnp.where(match, 1.0, 0.0).astype(BF16)


def dot(a, b):
    return jnp.dot(a, b, preferred_element_type=F32)


def dot_nt(a, b):
    return lax.dot_general(a, b, (((1,), (1,)), ((), ())), preferred_element_type=F32)


def earlier(lanes):
    return hot(iota((lanes, lanes), 0) < iota((lanes, lanes), 1))


def picking(limit):
    lane = iota((8 * PITCH, 8 * limit), 1)
    target = lane
    for i in range(1, 8):
        target = target + jnp.where(lane >= i * limit, PITCH - limit, 0)
    return hot(iota((8 * PITCH, 8 * limit), 0) == target)


def place(kind, valid, lanes, limit, before):
    classes = iota((8, lanes), 0)
    member = (kind == classes) & valid
    count = dot(hot(member), before)
    rank = jnp.sum(jnp.where(member, count, 0.0), axis=0, keepdims=True).astype(I32)
    kind, valid = kind[0:1], valid[0:1]
    slot = jnp.where(valid & (rank < limit), kind * limit + rank, -1)
    table = jnp.where(valid & (rank < limit), kind * PITCH + rank, -1)
    over = jnp.max(jnp.where(valid & (rank >= limit), 1.0, 0.0), axis=1, keepdims=True)
    return slot, table, over


def tabulate(code, table, over, lanes):
    sub = iota((8, lanes), 0)
    high, low = code >> 7, code & 127
    parts = jnp.where(sub == 0, high, jnp.where(sub == 1, low, 0)).astype(F32).astype(BF16)
    spread = hot(iota((8 * PITCH, lanes), 0) == table)
    return jnp.where(iota((8, 8 * PITCH), 0) == 2, over, dot_nt(parts, spread))


def flagged(table):
    return jnp.max(table[2:3], axis=1, keepdims=True)


def compacted(table, pick, column=False):
    if column:
        parts = lax.dot_general(
            pick, table.astype(BF16), (((0,), (1,)), ((), ())), preferred_element_type=F32
        )
        return (parts[:, 0:1] * 128.0 + parts[:, 1:2]).astype(I32)
    parts = dot(table.astype(BF16), pick)
    return (parts[0:1] * 128.0 + parts[1:2]).astype(I32)


def turned(matrix):
    n = matrix.shape[1]
    eye = hot(iota((n, n), 0) == iota((n, n), 1))
    return dot_nt(eye, matrix).astype(BF16)


def kernel(
    cap_y,
    cap_z,
    query,
    key,
    value,
    cotangent,
    route,
    arrival,
    lengths,
    prefix,
    owner,
    grad_query,
    grad_key,
    grad_value,
    grad_prefix,
    overflow,
    x_table_out,
    x_table,
    y_table_out,
    y_table_in,
    z_table_out,
    z_table_in,
    flag_out,
    flag_in,
    x_in,
    y_out,
    y_in,
    z_out,
    z_in,
    bz_out,
    bz_in,
    by_out,
    by_in,
    bx_out,
    pre_raw,
    pre_own,
    pre_in,
    pre_now,
    pre_far,
    to_y,
    to_z,
    to_rows,
    from_y,
    from_z,
    from_rows,
    mask,
    before_y,
    before_z,
    pick_y,
    acc,
    acc_in,
    chip,
    chip_in,
    total,
    total_in,
    t_send,
    t_recv,
    x_send,
    x_recv,
    y_send,
    y_recv,
    z_send,
    z_recv,
    bz_send,
    bz_recv,
    by_send,
    by_recv,
    bx_send,
    bx_recv,
    p_send,
    p_recv,
    a_send,
    a_recv,
):
    grp = lax.axis_index("grp")
    tp = lax.axis_index("tp")
    plane = grp // PLANE
    spot = lax.rem(grp, PLANE)
    core = lax.rem(spot, 2)
    side = lax.rem(spot // 2, 2)
    mate = grp + 1 - 2 * core
    across = grp + 2 - 4 * side

    def x_peer(k):
        return lax.rem(tp + k, TP)

    def y_peer(k):
        return lax.rem(spot + k, PLANE)

    def z_peer(k):
        return lax.rem(plane + k, PLANE)

    def at_x(k):
        return (grp, x_peer(k))

    def at_y(k):
        return (plane * PLANE + y_peer(k), tp)

    def at_z(k):
        return (z_peer(k) * PLANE + spot, tp)

    def block(index, size):
        return pl.ds(pl.multiple_of(index * size, size), size)

    def remote(src, dst, send, recv, device):
        copy = pltpu.make_async_remote_copy(
            src_ref=src,
            dst_ref=dst,
            send_sem=send,
            recv_sem=recv,
            device_id=device,
            device_id_type=MESH,
        )
        copy.start()
        return copy

    def local(src, dst, sem):
        pltpu.make_async_copy(src, dst, sem).start()

    def await_bytes(ref, sem):
        pltpu.make_async_copy(ref, ref, sem).wait()

    local(prefix.at[0], pre_raw, p_recv.at[3])
    entry = pltpu.get_barrier_semaphore()
    for k in range(1, TP):
        pl.semaphore_signal(entry, inc=1, device_id=at_x(k), device_id_type=MESH)
    for k in range(1, PLANE):
        pl.semaphore_signal(entry, inc=1, device_id=at_y(k), device_id_type=MESH)
    for k in range(1, PLANE):
        pl.semaphore_signal(entry, inc=1, device_id=at_z(k), device_id_type=MESH)
    before_y[...] = earlier(ROWS)
    before_z[...] = earlier(8 * cap_y)
    pick_y[...] = picking(cap_y)
    pl.semaphore_wait(entry, TP - 1 + 2 * (PLANE - 1))

    x_table_out[...] = jnp.broadcast_to(route[...].reshape(1, SEND), (8, SEND)).astype(F32)
    for k in range(1, TP):
        remote(x_table_out, x_table.at[k - 1], t_send.at[0], t_recv.at[0], at_x(k))

    def place_of(kind, head, device):
        per = KH if kind in "kv" else KH * RATIO
        return pl.multiple_of((device * per + head) * D, D)

    def x_stage(chunk):
        if chunk >= CHUNKS:
            return
        sources = {"q": query, "k": key, "v": value, "c": cotangent}
        for k in range(TP):
            to = x_peer(k)
            lane = 0
            for kind, head, heads in FORWARD[chunk]:
                src = sources[kind].at[:, pl.ds(place_of(kind, head, to), heads * D)]
                dst = x_in.at[chunk, block(tp, SEND), pl.ds(lane, heads * D)]
                if k == 0:
                    local(src, dst, x_recv.at[chunk])
                else:
                    remote(src, dst, x_send.at[chunk], x_recv.at[chunk], at_x(k))
                lane += heads * D

    for chunk in range(AHEAD):
        x_stage(chunk)

    await_bytes(pre_raw, p_recv.at[3])
    for kv in range(2):
        part = pre_raw[:, kv, :]
        for kh in range(KH):
            lower = (kv * KH + kh) * PRE
            pre_own[lower : lower + PRE] = part[:, kh * D : (kh + 1) * D]
    remote(pre_own, pre_in, p_send.at[0], p_recv.at[0], (mate, tp))

    await_bytes(x_table, t_recv.at[0])
    routes = jnp.zeros((8, ROWS), F32)
    for k in range(TP):
        begin = lax.rem(tp + TP - k, TP) * SEND
        spread = hot(iota((SEND, ROWS), 0) + begin == iota((SEND, ROWS), 1))
        heard = x_table_out[...] if k == 0 else x_table[k - 1]
        routes = routes + dot(heard.astype(BF16), spread)
    routes = routes.astype(I32)
    trainer = routes >> 1
    line = iota((8, ROWS), 1) // SEND
    number = grp * (2 * TP) + line * 2 + (routes & 1)
    code = ((trainer >> 3) * 512 + number + 1)[0:1]
    slot, table, over = place(trainer & 7, trainer >= 0, ROWS, cap_y, before_y[...])
    to_y[...] = hot(iota((8 * cap_y, ROWS), 0) == slot)
    y_table_out[...] = tabulate(code, table, over, ROWS)
    for k in range(1, PLANE):
        remote(
            y_table_out.at[:, block(y_peer(k), PITCH)],
            y_table_in.at[:, block(spot, PITCH)],
            t_send.at[1],
            t_recv.at[1],
            at_y(k),
        )
    local(
        y_table_out.at[:, block(spot, PITCH)], y_table_in.at[:, block(spot, PITCH)], t_recv.at[1]
    )

    def y_stage(chunk):
        wide = width(FORWARD[chunk])
        lanes = pl.ds(0, wide)
        await_bytes(x_in.at[chunk, :, lanes], x_recv.at[chunk])
        x_stage(chunk + AHEAD)
        y_out[chunk, :, 0:wide] = dot(to_y[...], x_in[chunk, :, 0:wide]).astype(BF16)
        for k in range(1, PLANE):
            remote(
                y_out.at[chunk, block(y_peer(k), cap_y), lanes],
                y_in.at[chunk, block(spot, cap_y), lanes],
                y_send.at[chunk],
                y_recv.at[chunk],
                at_y(k),
            )
        local(
            y_out.at[chunk, block(spot, cap_y), lanes],
            y_in.at[chunk, block(spot, cap_y), lanes],
            y_recv.at[chunk],
        )

    def z_stage(chunk):
        wide = width(FORWARD[chunk])
        lanes = pl.ds(0, wide)
        await_bytes(y_in.at[chunk, :, lanes], y_recv.at[chunk])
        z_out[chunk, :, 0:wide] = dot(to_z[...], y_in[chunk, :, 0:wide]).astype(BF16)
        for k in (4, 3, 5, 2, 6, 1, 7):
            remote(
                z_out.at[chunk, block(z_peer(k), cap_z), lanes],
                z_in.at[chunk, block(plane, cap_z), lanes],
                z_send.at[chunk],
                z_recv.at[chunk],
                at_z(k),
            )
        local(
            z_out.at[chunk, block(plane, cap_z), lanes],
            z_in.at[chunk, block(plane, cap_z), lanes],
            z_recv.at[chunk],
        )

    y_stage(0)
    y_stage(1)

    await_bytes(y_table_in, t_recv.at[1])
    code = compacted(y_table_in[...], pick_y[...])
    lanes = 8 * cap_y
    code8 = jnp.broadcast_to(code, (8, lanes))
    slot, table, over = place((code8 - 1) >> 9, code8 > 0, lanes, cap_z, before_z[...])
    to_z[...] = hot(iota((8 * cap_z, lanes), 0) == slot)
    z_stage(0)
    over = jnp.maximum(over, flagged(y_table_in[...]))
    z_table_out[...] = tabulate(((code - 1) & 511) + 1, table, over, lanes)
    for k in range(1, PLANE):
        remote(
            z_table_out.at[:, block(z_peer(k), PITCH)],
            z_table_in.at[:, block(plane, PITCH)],
            t_send.at[2],
            t_recv.at[2],
            at_z(k),
        )
    local(
        z_table_out.at[:, block(plane, PITCH)], z_table_in.at[:, block(plane, PITCH)], t_recv.at[2]
    )

    hold = owner[grp // TP]

    def prompt_across():
        await_bytes(pre_in, p_recv.at[0])
        mine = (hold & 1) == core
        pre_now[...] = jnp.where(mine, pre_own[...].astype(F32), pre_in[...].astype(F32)).astype(BF16)
        remote(
            pre_now.at[block(core, 2 * PRE)],
            pre_far.at[block(core, 2 * PRE)],
            p_send.at[1],
            p_recv.at[1],
            (across, tp),
        )

    def prompt_mate():
        await_bytes(pre_far.at[block(core, 2 * PRE)], p_recv.at[1])
        remote(
            pre_far.at[block(core, 2 * PRE)],
            pre_far.at[block(core, 2 * PRE)],
            p_send.at[2],
            p_recv.at[2],
            (mate, tp),
        )

    for chunk in range(2, CHUNKS):
        y_stage(chunk)
        z_stage(chunk - 1)
        if chunk == PROMPT:
            prompt_across()
    z_stage(CHUNKS - 1)
    prompt_mate()

    query_row = iota((ROWS, ROWS), 1)
    key_row = iota((ROWS, ROWS), 0)
    same = key_row <= query_row
    end = 0
    for i in range(3):
        end = end + lengths[0, i]
        same = same & ((key_row >= end) == (query_row >= end))
    mask[...] = jnp.where(same, 0.0, NEGATIVE)
    await_bytes(pre_far.at[block(1 - core, 2 * PRE)], p_recv.at[2])
    await_bytes(pre_now.at[pl.ds(0, 2 * PRE)], p_send.at[1])
    here = (hold >> 1) == side
    pre_now[...] = jnp.where(here, pre_now[...].astype(F32), pre_far[...].astype(F32)).astype(BF16)
    from_y[...] = turned(to_y[...])
    from_z[...] = turned(to_z[...])

    await_bytes(z_table_in, t_recv.at[2])
    flag_out[...] = jnp.broadcast_to(flagged(z_table_in[...]), (8, PITCH))
    for k in range(1, PLANE):
        remote(flag_out, flag_in.at[k - 1], t_send.at[3], t_recv.at[3], at_y(k))
    code = compacted(z_table_in[...], picking(cap_z), column=True) - 1
    rows = hot(code == arrival[...].reshape(1, ROWS))
    from_rows[...] = rows
    to_rows[...] = turned(rows)

    def back_z(chunk, result):
        wide = result.shape[1]
        lanes = pl.ds(0, wide)
        bz_out[chunk, :, 0:wide] = dot(from_rows[...], result).astype(BF16)
        for k in (4, 3, 5, 2, 6, 1, 7):
            remote(
                bz_out.at[chunk, block(z_peer(k), cap_z), lanes],
                bz_in.at[chunk, block(plane, cap_z), lanes],
                bz_send.at[chunk],
                bz_recv.at[chunk],
                at_z(k),
            )
        local(
            bz_out.at[chunk, block(plane, cap_z), lanes],
            bz_in.at[chunk, block(plane, cap_z), lanes],
            bz_recv.at[chunk],
        )

    def back_y(chunk):
        wide = width(BACKWARD[chunk])
        lanes = pl.ds(0, wide)
        await_bytes(bz_in.at[chunk, :, lanes], bz_recv.at[chunk])
        by_out[chunk, :, 0:wide] = dot(from_z[...], bz_in[chunk, :, 0:wide]).astype(BF16)
        for k in range(1, PLANE):
            remote(
                by_out.at[chunk, block(y_peer(k), cap_y), lanes],
                by_in.at[chunk, block(spot, cap_y), lanes],
                by_send.at[chunk],
                by_recv.at[chunk],
                at_y(k),
            )
        local(
            by_out.at[chunk, block(spot, cap_y), lanes],
            by_in.at[chunk, block(spot, cap_y), lanes],
            by_recv.at[chunk],
        )

    def back_x(chunk):
        wide = width(BACKWARD[chunk])
        lanes = pl.ds(0, wide)
        await_bytes(by_in.at[chunk, :, lanes], by_recv.at[chunk])
        bx_out[chunk, :, 0:wide] = dot(from_y[...], by_in[chunk, :, 0:wide]).astype(BF16)
        targets = {"q": grad_query, "k": grad_key, "v": grad_value}
        for k in range(TP):
            lane = 0
            for kind, head, heads in BACKWARD[chunk]:
                src = bx_out.at[chunk, block(x_peer(k), SEND), pl.ds(lane, heads * D)]
                dst = targets[kind].at[:, pl.ds(place_of(kind, head, tp), heads * D)]
                if k == 0:
                    local(src, dst, bx_recv.at[chunk])
                else:
                    remote(src, dst, bx_send.at[chunk], bx_recv.at[chunk], at_x(k))
                lane += heads * D

    def reduce_core(kh):
        remote(acc.at[kh, 1 - core], acc_in.at[kh], a_send.at[kh, 0], a_recv.at[kh, 0], (mate, tp))

    def reduce_side(kh):
        await_bytes(acc_in.at[kh], a_recv.at[kh, 0])
        chip[kh] = acc[kh, core] + acc_in[kh]
        remote(chip.at[kh], chip_in.at[kh], a_send.at[kh, 1], a_recv.at[kh, 1], (across, tp))

    def reduce_mate(kh):
        await_bytes(chip_in.at[kh], a_recv.at[kh, 1])
        total[kh] = chip[kh] + chip_in[kh]
        remote(total.at[kh], total_in.at[kh], a_send.at[kh, 2], a_recv.at[kh, 2], (mate, tp))

    def reduce_end(kh):
        await_bytes(total_in.at[kh], a_recv.at[kh, 2])
        mine, theirs = total[kh], total_in[kh]
        for kv in range(2):
            whole = jnp.where(core == kv, mine, theirs)
            whole = jnp.where(hold == 2 * side + core, whole, 0.0)
            grad_prefix[0, :, kv, kh * D : (kh + 1) * D] = whole

    def tokens(chunk):
        wide = width(FORWARD[chunk])
        await_bytes(z_in.at[chunk, :, pl.ds(0, wide)], z_recv.at[chunk])
        return dot(to_rows[...], z_in[chunk, :, 0:wide]).astype(BF16)

    def attend(keys, values, keys_t, queries, grads, key_grad, value_grad):
        scores = dot_nt(keys, queries) * SCALE
        scores = jnp.concatenate([scores[:PRE], scores[PRE:] + mask[...]], axis=0)
        weights = jnp.exp(scores - jnp.max(scores, axis=0, keepdims=True))
        probability = weights * (1.0 / jnp.sum(weights, axis=0, keepdims=True))
        grad_prob = dot_nt(values, grads)
        delta = jnp.sum(probability * grad_prob, axis=0, keepdims=True)
        dscore = (probability * (grad_prob - delta)).astype(BF16)
        key_part = dot(dscore, queries)
        value_part = dot(probability.astype(BF16), grads)
        query_grad = (jnp.transpose(dot(keys_t, dscore)) * SCALE).astype(BF16)
        if key_grad is None:
            return query_grad, key_part, value_part
        return query_grad, key_grad + key_part, value_grad + value_part

    arrived = {}

    def rows_of(kind, head):
        chunk, lane = found(FORWARD, kind, head)
        if chunk not in arrived:
            arrived[chunk] = tokens(chunk)
        return arrived[chunk][:, lane : lane + D]

    done = {}

    def finish(kind, head, value):
        done[kind, head] = value
        chunk, _ = found(BACKWARD, kind, head)
        names = [(k, h) for k, first, heads in BACKWARD[chunk] for h in range(first, first + heads)]
        if all(name in done for name in names):
            parts = [done[name] for name in names]
            back_z(chunk, parts[0] if len(parts) == 1 else jnp.concatenate(parts, axis=1))

    for kh in range(KH):
        lower = kh * PRE
        keys = jnp.concatenate([pre_now[lower : lower + PRE], rows_of("k", kh)], axis=0)
        values = jnp.concatenate(
            [pre_now[KH * PRE + lower : KH * PRE + lower + PRE], rows_of("v", kh)], axis=0
        )
        keys_t = jnp.transpose(keys.astype(F32)).astype(BF16)
        key_grad = value_grad = None
        for head in range(kh * RATIO, (kh + 1) * RATIO):
            result, key_grad, value_grad = attend(
                keys,
                values,
                keys_t,
                rows_of("q", head),
                rows_of("c", head),
                key_grad,
                value_grad,
            )
            finish("q", head, result)
        acc[kh, 0] = key_grad[:PRE] * SCALE
        acc[kh, 1] = value_grad[:PRE]
        reduce_core(kh)
        finish("k", kh, (key_grad[PRE:] * SCALE).astype(BF16))
        finish("v", kh, value_grad[PRE:].astype(BF16))
        if kh == 1:
            reduce_side(0)

    for step in range(BACKS + 2):
        if step < BACKS:
            back_y(step)
        if step >= 2:
            back_x(step - 2)
        if step == 2:
            reduce_side(1)
            reduce_mate(0)
        if step == 6:
            reduce_mate(1)
            reduce_end(0)
    reduce_end(1)
    await_bytes(flag_in, t_recv.at[3])
    overflow[0] = jnp.max(jnp.maximum(flag_out[...], jnp.max(flag_in[...], axis=0))).astype(I32)

    await_bytes(x_table, t_send.at[0])
    await_bytes(flag_in, t_send.at[3])
    for i, ref in ((1, y_table_out), (2, z_table_out)):
        await_bytes(ref.at[:, pl.ds(0, 7 * PITCH)], t_send.at[i])
    for chunk in range(CHUNKS):
        lanes = pl.ds(0, width(FORWARD[chunk]))
        await_bytes(x_in.at[chunk, pl.ds(0, 3 * SEND), lanes], x_send.at[chunk])
        await_bytes(y_out.at[chunk, pl.ds(0, 7 * cap_y), lanes], y_send.at[chunk])
        await_bytes(z_out.at[chunk, pl.ds(0, 7 * cap_z), lanes], z_send.at[chunk])
    for chunk in range(BACKS):
        lanes = pl.ds(0, width(BACKWARD[chunk]))
        await_bytes(bz_out.at[chunk, pl.ds(0, 7 * cap_z), lanes], bz_send.at[chunk])
        await_bytes(by_out.at[chunk, pl.ds(0, 7 * cap_y), lanes], by_send.at[chunk])
        await_bytes(bx_out.at[chunk, pl.ds(0, 3 * SEND), lanes], bx_send.at[chunk])
        await_bytes(bx_out.at[chunk, :, lanes], bx_recv.at[chunk])
    await_bytes(pre_own, p_send.at[0])
    await_bytes(pre_now.at[pl.ds(0, 2 * PRE)], p_send.at[2])
    for kh in range(KH):
        for i in range(3):
            await_bytes(chip.at[kh], a_send.at[kh, i])


def whole_step(cap_y, cap_z, number, operands):
    def vmem(*shape, dtype=BF16):
        return pltpu.VMEM(shape, dtype)

    dma = pltpu.SemaphoreType.DMA
    in_vmem = pl.BlockSpec(memory_space=pltpu.VMEM)
    in_smem = pl.BlockSpec(memory_space=pltpu.SMEM)
    in_hbm = pl.BlockSpec(memory_space=pltpu.HBM)
    anywhere = pl.BlockSpec(memory_space=pl.ANY)
    return pl.pallas_call(
        functools.partial(kernel, cap_y, cap_z),
        out_shape=(
            jax.ShapeDtypeStruct((SEND, TP * KH * RATIO * D), BF16),
            jax.ShapeDtypeStruct((SEND, TP * KH * D), BF16),
            jax.ShapeDtypeStruct((SEND, TP * KH * D), BF16),
            jax.ShapeDtypeStruct((1, PRE, 2, KH * D), F32),
            jax.ShapeDtypeStruct((1,), I32),
        ),
        in_specs=[in_hbm] * 4 + [in_vmem] * 2 + [in_smem, anywhere, in_smem],
        out_specs=(anywhere,) * 3 + (in_vmem, in_smem),
        scratch_shapes=[
            vmem(8, SEND, dtype=F32),
            vmem(TP - 1, 8, SEND, dtype=F32),
            vmem(8, 8 * PITCH, dtype=F32),
            vmem(8, 8 * PITCH, dtype=F32),
            vmem(8, 8 * PITCH, dtype=F32),
            vmem(8, 8 * PITCH, dtype=F32),
            vmem(8, PITCH, dtype=F32),
            vmem(PLANE - 1, 8, PITCH, dtype=F32),
            vmem(CHUNKS, ROWS, WIDE),
            vmem(CHUNKS, 8 * cap_y, WIDE),
            vmem(CHUNKS, 8 * cap_y, WIDE),
            vmem(CHUNKS, 8 * cap_z, WIDE),
            vmem(CHUNKS, 8 * cap_z, WIDE),
            vmem(BACKS, 8 * cap_z, BACK),
            vmem(BACKS, 8 * cap_z, BACK),
            vmem(BACKS, 8 * cap_y, BACK),
            vmem(BACKS, 8 * cap_y, BACK),
            vmem(BACKS, ROWS, BACK),
            vmem(PRE, 2, KH * D),
            vmem(2 * KH * PRE, D),
            vmem(2 * KH * PRE, D),
            vmem(2 * KH * PRE, D),
            vmem(2 * KH * PRE, D),
            vmem(8 * cap_y, ROWS),
            vmem(8 * cap_z, 8 * cap_y),
            vmem(ROWS, 8 * cap_z),
            vmem(ROWS, 8 * cap_y),
            vmem(8 * cap_y, 8 * cap_z),
            vmem(8 * cap_z, ROWS),
            vmem(ROWS, ROWS, dtype=F32),
            vmem(ROWS, ROWS),
            vmem(8 * cap_y, 8 * cap_y),
            vmem(8 * PITCH, 8 * cap_y),
            vmem(KH, 2, PRE, D, dtype=F32),
            vmem(KH, PRE, D, dtype=F32),
            vmem(KH, PRE, D, dtype=F32),
            vmem(KH, PRE, D, dtype=F32),
            vmem(KH, PRE, D, dtype=F32),
            vmem(KH, PRE, D, dtype=F32),
            dma((4,)),
            dma((4,)),
            dma((CHUNKS,)),
            dma((CHUNKS,)),
            dma((CHUNKS,)),
            dma((CHUNKS,)),
            dma((CHUNKS,)),
            dma((CHUNKS,)),
            dma((BACKS,)),
            dma((BACKS,)),
            dma((BACKS,)),
            dma((BACKS,)),
            dma((BACKS,)),
            dma((BACKS,)),
            dma((3,)),
            dma((4,)),
            dma((KH, 3)),
            dma((KH, 3)),
        ],
        compiler_params=pltpu.CompilerParams(
            collective_id=number, has_side_effects=True, vmem_limit_bytes=60 * 2**20
        ),
    )(*operands)


def hand_out(*refs):
    sources, targets, sem = refs[:4], refs[4:8], refs[8]
    copies = [
        pltpu.make_async_copy(source, target, sem.at[i])
        for i, (source, target) in enumerate(zip(sources, targets))
    ]
    for copy in copies:
        copy.start()
    for copy in copies:
        copy.wait()


def handed_out(results):
    anywhere = pl.BlockSpec(memory_space=pl.ANY)
    return pl.pallas_call(
        hand_out,
        out_shape=tuple(jax.ShapeDtypeStruct(x.shape, x.dtype) for x in results),
        in_specs=[anywhere] * 4,
        out_specs=(anywhere,) * 4,
        scratch_shapes=[pltpu.SemaphoreType.DMA((4,))],
    )(*results)


def body(
    roll_query, roll_key, roll_value, roll_cotangent, route, arrival, lengths, prefix_kv, owner
):
    operands = (
        roll_query,
        roll_key,
        roll_value,
        roll_cotangent,
        route,
        arrival,
        lengths,
        prefix_kv,
        owner,
    )
    *quick, overflow = whole_step(48, 48, 0, operands)
    results = lax.cond(
        overflow[0] > 0,
        lambda: tuple(whole_step(64, 64, 1, operands)[:4]),
        lambda: tuple(quick),
    )
    return handed_out(results)


def solution(mesh):
    return jax.shard_map(
        body,
        mesh=mesh,
        in_specs=(
            P(("grp", "tp"), None),
            P(("grp", "tp"), None),
            P(("grp", "tp"), None),
            P(("grp", "tp"), None),
            P(("grp", "tp")),
            P("grp"),
            P("grp", None),
            P("grp", None, None, "tp"),
            P(),
        ),
        out_specs=(
            P(("grp", "tp"), None),
            P(("grp", "tp"), None),
            P(("grp", "tp"), None),
            P("grp", None, None, "tp"),
        ),
        check_vma=False,
    )
```

```python
import functools
import math

import jax
import jax.numpy as jnp
from jax import lax
from jax.experimental import pallas as pl
from jax.experimental.pallas import tpu as pltpu
from jax.sharding import PartitionSpec as P

MESH = pl.DeviceIdType.MESH
D = 128
TP = 4
PLANE = 8
RATIO = 5
KH = 2
ROWS = 256
SEND = 64
PRE = 512
FORWARD = (
    (("k", 0, 1),),
    (("v", 0, 1), ("q", 0, 1)),
    (("c", 0, 1),),
    (("q", 1, 2), ("c", 1, 2)),
    (("q", 3, 2), ("c", 3, 2)),
    (("k", 1, 1), ("v", 1, 1), ("q", 5, 1), ("c", 5, 1)),
    (("q", 6, 2), ("c", 6, 2)),
    (("q", 8, 1), ("c", 8, 1)),
    (("q", 9, 1), ("c", 9, 1)),
)
BACKWARD = (
    (("q", 0, 1),),
    (("q", 1, 2),),
    (("q", 3, 2),),
    (("k", 0, 1), ("v", 0, 1)),
    (("q", 5, 1),),
    (("q", 6, 2),),
    (("q", 8, 1),),
    (("q", 9, 1),),
    (("k", 1, 1),),
    (("v", 1, 1),),
)
CHUNKS = len(FORWARD)
BACKS = len(BACKWARD)
WIDE = 512
BACK = 256
PITCH = 128
NEGATIVE = -1e30
SCALE = 1.0 / math.sqrt(D)
F32 = jnp.float32
BF16 = jnp.bfloat16
I32 = jnp.int32
AHEAD = 2
PROMPT = 5


def width(chunk):
    return D * sum(heads for _, _, heads in chunk)


def found(chunks, kind, head):
    for number, chunk in enumerate(chunks):
        lane = 0
        for name, first, heads in chunk:
            if name == kind and first <= head < first + heads:
                return number, lane + (head - first) * D
            lane += heads * D


def iota(shape, dim):
    return lax.broadcasted_iota(I32, shape, dim)


def hot(match):
    return jnp.where(match, 1.0, 0.0).astype(BF16)


def dot(a, b):
    return jnp.dot(a, b, preferred_element_type=F32)


def dot_nt(a, b):
    return lax.dot_general(a, b, (((1,), (1,)), ((), ())), preferred_element_type=F32)


def earlier(lanes):
    return hot(iota((lanes, lanes), 0) < iota((lanes, lanes), 1))


def picking(limit):
    lane = iota((8 * PITCH, 8 * limit), 1)
    target = lane
    for i in range(1, 8):
        target = target + jnp.where(lane >= i * limit, PITCH - limit, 0)
    return hot(iota((8 * PITCH, 8 * limit), 0) == target)


def place(kind, valid, lanes, limit, before):
    classes = iota((8, lanes), 0)
    member = (kind == classes) & valid
    count = dot(hot(member), before)
    rank = jnp.sum(jnp.where(member, count, 0.0), axis=0, keepdims=True).astype(I32)
    kind, valid = kind[0:1], valid[0:1]
    slot = jnp.where(valid & (rank < limit), kind * limit + rank, -1)
    table = jnp.where(valid & (rank < limit), kind * PITCH + rank, -1)
    over = jnp.max(jnp.where(valid & (rank >= limit), 1.0, 0.0), axis=1, keepdims=True)
    return slot, table, over


def tabulate(code, table, over, lanes):
    sub = iota((8, lanes), 0)
    high, low = code >> 7, code & 127
    parts = jnp.where(sub == 0, high, jnp.where(sub == 1, low, 0)).astype(F32).astype(BF16)
    spread = hot(iota((8 * PITCH, lanes), 0) == table)
    return jnp.where(iota((8, 8 * PITCH), 0) == 2, over, dot_nt(parts, spread))


def flagged(table):
    return jnp.max(table[2:3], axis=1, keepdims=True)


def compacted(table, pick, column=False):
    if column:
        parts = lax.dot_general(
            pick, table.astype(BF16), (((0,), (1,)), ((), ())), preferred_element_type=F32
        )
        return (parts[:, 0:1] * 128.0 + parts[:, 1:2]).astype(I32)
    parts = dot(table.astype(BF16), pick)
    return (parts[0:1] * 128.0 + parts[1:2]).astype(I32)


def turned(matrix):
    n = matrix.shape[1]
    eye = hot(iota((n, n), 0) == iota((n, n), 1))
    return dot_nt(eye, matrix).astype(BF16)


def kernel(
    cap_y,
    cap_z,
    query,
    key,
    value,
    cotangent,
    route,
    arrival,
    lengths,
    prefix,
    owner,
    grad_query,
    grad_key,
    grad_value,
    grad_prefix,
    overflow,
    x_table_out,
    x_table,
    y_table_out,
    y_table_in,
    z_table_out,
    z_table_in,
    flag_out,
    flag_in,
    x_in,
    y_out,
    y_in,
    z_out,
    z_in,
    bz_out,
    bz_in,
    by_out,
    by_in,
    bx_out,
    pre_raw,
    pre_own,
    pre_in,
    pre_now,
    pre_far,
    to_y,
    to_z,
    to_rows,
    from_y,
    from_z,
    from_rows,
    mask,
    before_y,
    before_z,
    pick_y,
    acc,
    acc_in,
    chip,
    chip_out,
    chip_in,
    total,
    total_in,
    t_send,
    t_recv,
    x_send,
    x_recv,
    y_send,
    y_recv,
    z_send,
    z_recv,
    bz_send,
    bz_recv,
    by_send,
    by_recv,
    bx_send,
    bx_recv,
    p_send,
    p_recv,
    a_send,
    a_recv,
):
    grp = lax.axis_index("grp")
    tp = lax.axis_index("tp")
    plane = grp // PLANE
    spot = lax.rem(grp, PLANE)
    core = lax.rem(spot, 2)
    side = lax.rem(spot // 2, 2)
    mate = grp + 1 - 2 * core
    across = grp + 2 - 4 * side

    def x_peer(k):
        return lax.rem(tp + k, TP)

    def y_peer(k):
        return lax.rem(spot + k, PLANE)

    def z_peer(k):
        return lax.rem(plane + k, PLANE)

    def at_x(k):
        return (grp, x_peer(k))

    def at_y(k):
        return (plane * PLANE + y_peer(k), tp)

    def at_z(k):
        return (z_peer(k) * PLANE + spot, tp)

    def block(index, size):
        return pl.ds(pl.multiple_of(index * size, size), size)

    def remote(src, dst, send, recv, device):
        copy = pltpu.make_async_remote_copy(
            src_ref=src,
            dst_ref=dst,
            send_sem=send,
            recv_sem=recv,
            device_id=device,
            device_id_type=MESH,
        )
        copy.start()
        return copy

    def local(src, dst, sem):
        pltpu.make_async_copy(src, dst, sem).start()

    def await_bytes(ref, sem):
        pltpu.make_async_copy(ref, ref, sem).wait()

    local(prefix.at[0], pre_raw, p_recv.at[3])
    entry = pltpu.get_barrier_semaphore()
    for k in range(1, TP):
        pl.semaphore_signal(entry, inc=1, device_id=at_x(k), device_id_type=MESH)
    for k in range(1, PLANE):
        pl.semaphore_signal(entry, inc=1, device_id=at_y(k), device_id_type=MESH)
    for k in range(1, PLANE):
        pl.semaphore_signal(entry, inc=1, device_id=at_z(k), device_id_type=MESH)
    before_y[...] = earlier(ROWS)
    before_z[...] = earlier(8 * cap_y)
    pick_y[...] = picking(cap_y)
    pl.semaphore_wait(entry, TP - 1 + 2 * (PLANE - 1))

    x_table_out[...] = jnp.broadcast_to(route[...].reshape(1, SEND), (8, SEND)).astype(F32)
    for k in range(1, TP):
        remote(x_table_out, x_table.at[k - 1], t_send.at[0], t_recv.at[0], at_x(k))

    def place_of(kind, head, device):
        per = KH if kind in "kv" else KH * RATIO
        return pl.multiple_of((device * per + head) * D, D)

    def x_stage(chunk):
        if chunk >= CHUNKS:
            return
        sources = {"q": query, "k": key, "v": value, "c": cotangent}
        for k in range(TP):
            to = x_peer(k)
            lane = 0
            for kind, head, heads in FORWARD[chunk]:
                src = sources[kind].at[:, pl.ds(place_of(kind, head, to), heads * D)]
                dst = x_in.at[chunk, block(tp, SEND), pl.ds(lane, heads * D)]
                if k == 0:
                    local(src, dst, x_recv.at[chunk])
                else:
                    remote(src, dst, x_send.at[chunk], x_recv.at[chunk], at_x(k))
                lane += heads * D

    for chunk in range(AHEAD):
        x_stage(chunk)

    await_bytes(pre_raw, p_recv.at[3])
    for kv in range(2):
        part = pre_raw[:, kv, :]
        for kh in range(KH):
            lower = (kv * KH + kh) * PRE
            pre_own[lower : lower + PRE] = part[:, kh * D : (kh + 1) * D]
    remote(pre_own, pre_in, p_send.at[0], p_recv.at[0], (mate, tp))

    await_bytes(x_table, t_recv.at[0])
    routes = jnp.zeros((8, ROWS), F32)
    for k in range(TP):
        begin = lax.rem(tp + TP - k, TP) * SEND
        spread = hot(iota((SEND, ROWS), 0) + begin == iota((SEND, ROWS), 1))
        heard = x_table_out[...] if k == 0 else x_table[k - 1]
        routes = routes + dot(heard.astype(BF16), spread)
    routes = routes.astype(I32)
    trainer = routes >> 1
    line = iota((8, ROWS), 1) // SEND
    number = grp * (2 * TP) + line * 2 + (routes & 1)
    code = ((trainer >> 3) * 512 + number + 1)[0:1]
    slot, table, over = place(trainer & 7, trainer >= 0, ROWS, cap_y, before_y[...])
    to_y[...] = hot(iota((8 * cap_y, ROWS), 0) == slot)
    y_table_out[...] = tabulate(code, table, over, ROWS)
    for k in range(1, PLANE):
        remote(
            y_table_out.at[:, block(y_peer(k), PITCH)],
            y_table_in.at[:, block(spot, PITCH)],
            t_send.at[1],
            t_recv.at[1],
            at_y(k),
        )
    local(
        y_table_out.at[:, block(spot, PITCH)], y_table_in.at[:, block(spot, PITCH)], t_recv.at[1]
    )

    def y_stage(chunk):
        wide = width(FORWARD[chunk])
        lanes = pl.ds(0, wide)
        await_bytes(x_in.at[chunk, :, lanes], x_recv.at[chunk])
        x_stage(chunk + AHEAD)
        y_out[chunk, :, 0:wide] = dot(to_y[...], x_in[chunk, :, 0:wide]).astype(BF16)
        for k in range(1, PLANE):
            remote(
                y_out.at[chunk, block(y_peer(k), cap_y), lanes],
                y_in.at[chunk, block(spot, cap_y), lanes],
                y_send.at[chunk],
                y_recv.at[chunk],
                at_y(k),
            )
        local(
            y_out.at[chunk, block(spot, cap_y), lanes],
            y_in.at[chunk, block(spot, cap_y), lanes],
            y_recv.at[chunk],
        )

    def z_stage(chunk):
        wide = width(FORWARD[chunk])
        lanes = pl.ds(0, wide)
        await_bytes(y_in.at[chunk, :, lanes], y_recv.at[chunk])
        z_out[chunk, :, 0:wide] = dot(to_z[...], y_in[chunk, :, 0:wide]).astype(BF16)
        for k in (4, 3, 5, 2, 6, 1, 7):
            remote(
                z_out.at[chunk, block(z_peer(k), cap_z), lanes],
                z_in.at[chunk, block(plane, cap_z), lanes],
                z_send.at[chunk],
                z_recv.at[chunk],
                at_z(k),
            )
        local(
            z_out.at[chunk, block(plane, cap_z), lanes],
            z_in.at[chunk, block(plane, cap_z), lanes],
            z_recv.at[chunk],
        )

    y_stage(0)
    y_stage(1)

    await_bytes(y_table_in, t_recv.at[1])
    code = compacted(y_table_in[...], pick_y[...])
    lanes = 8 * cap_y
    code8 = jnp.broadcast_to(code, (8, lanes))
    slot, table, over = place((code8 - 1) >> 9, code8 > 0, lanes, cap_z, before_z[...])
    to_z[...] = hot(iota((8 * cap_z, lanes), 0) == slot)
    z_stage(0)
    over = jnp.maximum(over, flagged(y_table_in[...]))
    z_table_out[...] = tabulate(((code - 1) & 511) + 1, table, over, lanes)
    for k in range(1, PLANE):
        remote(
            z_table_out.at[:, block(z_peer(k), PITCH)],
            z_table_in.at[:, block(plane, PITCH)],
            t_send.at[2],
            t_recv.at[2],
            at_z(k),
        )
    local(
        z_table_out.at[:, block(plane, PITCH)], z_table_in.at[:, block(plane, PITCH)], t_recv.at[2]
    )

    hold = owner[grp // TP]

    def prompt_across():
        await_bytes(pre_in, p_recv.at[0])
        mine = (hold & 1) == core
        pre_now[...] = jnp.where(mine, pre_own[...].astype(F32), pre_in[...].astype(F32)).astype(BF16)
        remote(
            pre_now.at[block(core, 2 * PRE)],
            pre_far.at[block(core, 2 * PRE)],
            p_send.at[1],
            p_recv.at[1],
            (across, tp),
        )

    def prompt_mate():
        await_bytes(pre_far.at[block(core, 2 * PRE)], p_recv.at[1])
        remote(
            pre_far.at[block(core, 2 * PRE)],
            pre_far.at[block(core, 2 * PRE)],
            p_send.at[2],
            p_recv.at[2],
            (mate, tp),
        )

    for chunk in range(2, CHUNKS):
        y_stage(chunk)
        z_stage(chunk - 1)
        if chunk == PROMPT:
            prompt_across()
    z_stage(CHUNKS - 1)
    prompt_mate()

    query_row = iota((ROWS, ROWS), 1)
    key_row = iota((ROWS, ROWS), 0)
    same = key_row <= query_row
    end = 0
    for i in range(3):
        end = end + lengths[0, i]
        same = same & ((key_row >= end) == (query_row >= end))
    mask[...] = jnp.where(same, 0.0, NEGATIVE)
    await_bytes(pre_far.at[block(1 - core, 2 * PRE)], p_recv.at[2])
    await_bytes(pre_now.at[pl.ds(0, 2 * PRE)], p_send.at[1])
    here = (hold >> 1) == side
    pre_now[...] = jnp.where(here, pre_now[...].astype(F32), pre_far[...].astype(F32)).astype(BF16)
    from_y[...] = turned(to_y[...])
    from_z[...] = turned(to_z[...])

    await_bytes(z_table_in, t_recv.at[2])
    flag_out[...] = jnp.broadcast_to(flagged(z_table_in[...]), (8, PITCH))
    for k in range(1, PLANE):
        remote(flag_out, flag_in.at[k - 1], t_send.at[3], t_recv.at[3], at_y(k))
    code = compacted(z_table_in[...], picking(cap_z), column=True) - 1
    rows = hot(code == arrival[...].reshape(1, ROWS))
    from_rows[...] = rows
    to_rows[...] = turned(rows)

    def back_z(chunk, result):
        wide = result.shape[1]
        lanes = pl.ds(0, wide)
        bz_out[chunk, :, 0:wide] = dot(from_rows[...], result).astype(BF16)
        for k in (4, 3, 5, 2, 6, 1, 7):
            remote(
                bz_out.at[chunk, block(z_peer(k), cap_z), lanes],
                bz_in.at[chunk, block(plane, cap_z), lanes],
                bz_send.at[chunk],
                bz_recv.at[chunk],
                at_z(k),
            )
        local(
            bz_out.at[chunk, block(plane, cap_z), lanes],
            bz_in.at[chunk, block(plane, cap_z), lanes],
            bz_recv.at[chunk],
        )

    def back_y(chunk):
        wide = width(BACKWARD[chunk])
        lanes = pl.ds(0, wide)
        await_bytes(bz_in.at[chunk, :, lanes], bz_recv.at[chunk])
        by_out[chunk, :, 0:wide] = dot(from_z[...], bz_in[chunk, :, 0:wide]).astype(BF16)
        for k in range(1, PLANE):
            remote(
                by_out.at[chunk, block(y_peer(k), cap_y), lanes],
                by_in.at[chunk, block(spot, cap_y), lanes],
                by_send.at[chunk],
                by_recv.at[chunk],
                at_y(k),
            )
        local(
            by_out.at[chunk, block(spot, cap_y), lanes],
            by_in.at[chunk, block(spot, cap_y), lanes],
            by_recv.at[chunk],
        )

    def back_x(chunk):
        wide = width(BACKWARD[chunk])
        lanes = pl.ds(0, wide)
        await_bytes(by_in.at[chunk, :, lanes], by_recv.at[chunk])
        bx_out[chunk, :, 0:wide] = dot(from_y[...], by_in[chunk, :, 0:wide]).astype(BF16)
        targets = {"q": grad_query, "k": grad_key, "v": grad_value}
        for k in range(TP):
            lane = 0
            for kind, head, heads in BACKWARD[chunk]:
                src = bx_out.at[chunk, block(x_peer(k), SEND), pl.ds(lane, heads * D)]
                dst = targets[kind].at[:, pl.ds(place_of(kind, head, tp), heads * D)]
                if k == 0:
                    local(src, dst, bx_recv.at[chunk])
                else:
                    remote(src, dst, bx_send.at[chunk], bx_recv.at[chunk], at_x(k))
                lane += heads * D

    def reduce_core(kh):
        remote(acc.at[kh, 1 - core], acc_in.at[kh], a_send.at[kh, 0], a_recv.at[kh, 0], (mate, tp))

    def reduce_side(kh):
        await_bytes(acc_in.at[kh], a_recv.at[kh, 0])
        chip[kh] = acc[kh, core] + acc_in[kh]
        chip_out[kh] = chip[kh].astype(BF16)
        remote(chip_out.at[kh], chip_in.at[kh], a_send.at[kh, 1], a_recv.at[kh, 1], (across, tp))

    def reduce_mate(kh):
        await_bytes(chip_in.at[kh], a_recv.at[kh, 1])
        total[kh] = chip[kh] + chip_in[kh].astype(F32)
        remote(total.at[kh], total_in.at[kh], a_send.at[kh, 2], a_recv.at[kh, 2], (mate, tp))

    def reduce_end(kh):
        await_bytes(total_in.at[kh], a_recv.at[kh, 2])
        mine, theirs = total[kh], total_in[kh]
        for kv in range(2):
            whole = jnp.where(core == kv, mine, theirs)
            whole = jnp.where(hold == 2 * side + core, whole, 0.0)
            grad_prefix[0, :, kv, kh * D : (kh + 1) * D] = whole

    def tokens(chunk):
        wide = width(FORWARD[chunk])
        await_bytes(z_in.at[chunk, :, pl.ds(0, wide)], z_recv.at[chunk])
        return dot(to_rows[...], z_in[chunk, :, 0:wide]).astype(BF16)

    def attend(keys, values, keys_t, queries, grads, key_grad, value_grad):
        scores = dot_nt(keys, queries) * SCALE
        scores = jnp.concatenate([scores[:PRE], scores[PRE:] + mask[...]], axis=0)
        weights = jnp.exp(scores - jnp.max(scores, axis=0, keepdims=True))
        probability = weights * (1.0 / jnp.sum(weights, axis=0, keepdims=True))
        grad_prob = dot_nt(values, grads)
        delta = jnp.sum(probability * grad_prob, axis=0, keepdims=True)
        dscore = (probability * (grad_prob - delta)).astype(BF16)
        key_part = dot(dscore, queries)
        value_part = dot(probability.astype(BF16), grads)
        query_grad = (jnp.transpose(dot(keys_t, dscore)) * SCALE).astype(BF16)
        if key_grad is None:
            return query_grad, key_part, value_part
        return query_grad, key_grad + key_part, value_grad + value_part

    arrived = {}

    def rows_of(kind, head):
        chunk, lane = found(FORWARD, kind, head)
        if chunk not in arrived:
            arrived[chunk] = tokens(chunk)
        return arrived[chunk][:, lane : lane + D]

    done = {}

    def finish(kind, head, value):
        done[kind, head] = value
        chunk, _ = found(BACKWARD, kind, head)
        names = [(k, h) for k, first, heads in BACKWARD[chunk] for h in range(first, first + heads)]
        if all(name in done for name in names):
            parts = [done[name] for name in names]
            back_z(chunk, parts[0] if len(parts) == 1 else jnp.concatenate(parts, axis=1))

    for kh in range(KH):
        lower = kh * PRE
        keys = jnp.concatenate([pre_now[lower : lower + PRE], rows_of("k", kh)], axis=0)
        values = jnp.concatenate(
            [pre_now[KH * PRE + lower : KH * PRE + lower + PRE], rows_of("v", kh)], axis=0
        )
        keys_t = jnp.transpose(keys.astype(F32)).astype(BF16)
        key_grad = value_grad = None
        for head in range(kh * RATIO, (kh + 1) * RATIO):
            result, key_grad, value_grad = attend(
                keys,
                values,
                keys_t,
                rows_of("q", head),
                rows_of("c", head),
                key_grad,
                value_grad,
            )
            finish("q", head, result)
        acc[kh, 0] = key_grad[:PRE] * SCALE
        acc[kh, 1] = value_grad[:PRE]
        reduce_core(kh)
        finish("k", kh, (key_grad[PRE:] * SCALE).astype(BF16))
        finish("v", kh, value_grad[PRE:].astype(BF16))
        if kh == 1:
            reduce_side(0)

    for step in range(BACKS + 2):
        if step < BACKS:
            back_y(step)
        if step >= 2:
            back_x(step - 2)
        if step == 2:
            reduce_side(1)
            reduce_mate(0)
        if step == 6:
            reduce_mate(1)
            reduce_end(0)
    reduce_end(1)
    await_bytes(flag_in, t_recv.at[3])
    overflow[0] = jnp.max(jnp.maximum(flag_out[...], jnp.max(flag_in[...], axis=0))).astype(I32)

    await_bytes(x_table, t_send.at[0])
    await_bytes(flag_in, t_send.at[3])
    for i, ref in ((1, y_table_out), (2, z_table_out)):
        await_bytes(ref.at[:, pl.ds(0, 7 * PITCH)], t_send.at[i])
    for chunk in range(CHUNKS):
        lanes = pl.ds(0, width(FORWARD[chunk]))
        await_bytes(x_in.at[chunk, pl.ds(0, 3 * SEND), lanes], x_send.at[chunk])
        await_bytes(y_out.at[chunk, pl.ds(0, 7 * cap_y), lanes], y_send.at[chunk])
        await_bytes(z_out.at[chunk, pl.ds(0, 7 * cap_z), lanes], z_send.at[chunk])
    for chunk in range(BACKS):
        lanes = pl.ds(0, width(BACKWARD[chunk]))
        await_bytes(bz_out.at[chunk, pl.ds(0, 7 * cap_z), lanes], bz_send.at[chunk])
        await_bytes(by_out.at[chunk, pl.ds(0, 7 * cap_y), lanes], by_send.at[chunk])
        await_bytes(bx_out.at[chunk, pl.ds(0, 3 * SEND), lanes], bx_send.at[chunk])
        await_bytes(bx_out.at[chunk, :, lanes], bx_recv.at[chunk])
    await_bytes(pre_own, p_send.at[0])
    await_bytes(pre_now.at[pl.ds(0, 2 * PRE)], p_send.at[2])
    for kh in range(KH):
        await_bytes(chip.at[kh], a_send.at[kh, 0])
        await_bytes(chip_out.at[kh], a_send.at[kh, 1])
        await_bytes(chip.at[kh], a_send.at[kh, 2])


def whole_step(cap_y, cap_z, number, operands):
    def vmem(*shape, dtype=BF16):
        return pltpu.VMEM(shape, dtype)

    dma = pltpu.SemaphoreType.DMA
    in_vmem = pl.BlockSpec(memory_space=pltpu.VMEM)
    in_smem = pl.BlockSpec(memory_space=pltpu.SMEM)
    in_hbm = pl.BlockSpec(memory_space=pltpu.HBM)
    anywhere = pl.BlockSpec(memory_space=pl.ANY)
    return pl.pallas_call(
        functools.partial(kernel, cap_y, cap_z),
        out_shape=(
            jax.ShapeDtypeStruct((SEND, TP * KH * RATIO * D), BF16),
            jax.ShapeDtypeStruct((SEND, TP * KH * D), BF16),
            jax.ShapeDtypeStruct((SEND, TP * KH * D), BF16),
            jax.ShapeDtypeStruct((1, PRE, 2, KH * D), F32),
            jax.ShapeDtypeStruct((1,), I32),
        ),
        in_specs=[in_hbm] * 4 + [in_vmem] * 2 + [in_smem, anywhere, in_smem],
        out_specs=(anywhere,) * 3 + (in_vmem, in_smem),
        scratch_shapes=[
            vmem(8, SEND, dtype=F32),
            vmem(TP - 1, 8, SEND, dtype=F32),
            vmem(8, 8 * PITCH, dtype=F32),
            vmem(8, 8 * PITCH, dtype=F32),
            vmem(8, 8 * PITCH, dtype=F32),
            vmem(8, 8 * PITCH, dtype=F32),
            vmem(8, PITCH, dtype=F32),
            vmem(PLANE - 1, 8, PITCH, dtype=F32),
            vmem(CHUNKS, ROWS, WIDE),
            vmem(CHUNKS, 8 * cap_y, WIDE),
            vmem(CHUNKS, 8 * cap_y, WIDE),
            vmem(CHUNKS, 8 * cap_z, WIDE),
            vmem(CHUNKS, 8 * cap_z, WIDE),
            vmem(BACKS, 8 * cap_z, BACK),
            vmem(BACKS, 8 * cap_z, BACK),
            vmem(BACKS, 8 * cap_y, BACK),
            vmem(BACKS, 8 * cap_y, BACK),
            vmem(BACKS, ROWS, BACK),
            vmem(PRE, 2, KH * D),
            vmem(2 * KH * PRE, D),
            vmem(2 * KH * PRE, D),
            vmem(2 * KH * PRE, D),
            vmem(2 * KH * PRE, D),
            vmem(8 * cap_y, ROWS),
            vmem(8 * cap_z, 8 * cap_y),
            vmem(ROWS, 8 * cap_z),
            vmem(ROWS, 8 * cap_y),
            vmem(8 * cap_y, 8 * cap_z),
            vmem(8 * cap_z, ROWS),
            vmem(ROWS, ROWS, dtype=F32),
            vmem(ROWS, ROWS),
            vmem(8 * cap_y, 8 * cap_y),
            vmem(8 * PITCH, 8 * cap_y),
            vmem(KH, 2, PRE, D, dtype=F32),
            vmem(KH, PRE, D, dtype=F32),
            vmem(KH, PRE, D, dtype=F32),
            vmem(KH, PRE, D),
            vmem(KH, PRE, D),
            vmem(KH, PRE, D, dtype=F32),
            vmem(KH, PRE, D, dtype=F32),
            dma((4,)),
            dma((4,)),
            dma((CHUNKS,)),
            dma((CHUNKS,)),
            dma((CHUNKS,)),
            dma((CHUNKS,)),
            dma((CHUNKS,)),
            dma((CHUNKS,)),
            dma((BACKS,)),
            dma((BACKS,)),
            dma((BACKS,)),
            dma((BACKS,)),
            dma((BACKS,)),
            dma((BACKS,)),
            dma((3,)),
            dma((4,)),
            dma((KH, 3)),
            dma((KH, 3)),
        ],
        compiler_params=pltpu.CompilerParams(
            collective_id=number, has_side_effects=True, vmem_limit_bytes=60 * 2**20
        ),
    )(*operands)


def hand_out(*refs):
    sources, targets, sem = refs[:4], refs[4:8], refs[8]
    copies = [
        pltpu.make_async_copy(source, target, sem.at[i])
        for i, (source, target) in enumerate(zip(sources, targets))
    ]
    for copy in copies:
        copy.start()
    for copy in copies:
        copy.wait()


def handed_out(results):
    anywhere = pl.BlockSpec(memory_space=pl.ANY)
    return pl.pallas_call(
        hand_out,
        out_shape=tuple(jax.ShapeDtypeStruct(x.shape, x.dtype) for x in results),
        in_specs=[anywhere] * 4,
        out_specs=(anywhere,) * 4,
        scratch_shapes=[pltpu.SemaphoreType.DMA((4,))],
    )(*results)


def body(
    roll_query, roll_key, roll_value, roll_cotangent, route, arrival, lengths, prefix_kv, owner
):
    operands = (
        roll_query,
        roll_key,
        roll_value,
        roll_cotangent,
        route,
        arrival,
        lengths,
        prefix_kv,
        owner,
    )
    *quick, overflow = whole_step(48, 48, 0, operands)
    results = lax.cond(
        overflow[0] > 0,
        lambda: tuple(whole_step(64, 64, 1, operands)[:4]),
        lambda: tuple(quick),
    )
    return handed_out(results)


def solution(mesh):
    return jax.shard_map(
        body,
        mesh=mesh,
        in_specs=(
            P(("grp", "tp"), None),
            P(("grp", "tp"), None),
            P(("grp", "tp"), None),
            P(("grp", "tp"), None),
            P(("grp", "tp")),
            P("grp"),
            P("grp", None),
            P("grp", None, None, "tp"),
            P(),
        ),
        out_specs=(
            P(("grp", "tp"), None),
            P(("grp", "tp"), None),
            P(("grp", "tp"), None),
            P("grp", None, None, "tp"),
        ),
        check_vma=False,
    )
```
